128 devices in a mesh: blk: 32 (over y, z, core), face: 4 (over x).
Axes of the slice: x: 4, y: 4, z: 4, core: 2. Of those that a mesh axis runs over, the one named last changes fastest.
Arguments:
- forcing: float32 [32, 4, 3, 64, 4096], P('blk', 'face'), may hold values from -6 to 6
- modulus: float32 [32, 4, 3], P('blk', 'face'), may hold values from 0.5 to 4
- orient_codes: int32 [32, 4], P('blk', 'face'), may hold values from 0 to 3
Outputs:
- displacement: float32 [32, 4, 3, 64, 4096], P('blk', 'face')
The draws below stay inside these ranges and needn't reach their ends.
All inputs are finite; a program needn't handle non-finite values.
Results may differ from the reference program's by a relative error of at most 0.0001.
Values sent between devices are 32-bit elements; how exact they have to be, the bound alone decides.
A program may use at most 128 MiB of HBM per device.

```python
import math
import jax
import jax.numpy as jnp
from jax import lax

NODES = 64
ITERS = 2
NBX = 32
NBY = 4


def plant(entries, stream_key, low, high):
    index_at = [jax.random.randint(jax.random.fold_in(stream_key, axis), (), 0, length) for axis, length in enumerate(entries.shape)]
    longest = entries.shape.index(max(entries.shape))
    next_to = index_at[:longest] + [(index_at[longest] + 1) % entries.shape[longest]] + index_at[longest + 1:]
    return entries.at[tuple(index_at)].set(low).at[tuple(next_to)].set(high)


def shard_levels(rng, dims, split, least, high):
    loudness = 1.0
    for dim, parts in split:
        heights = jax.random.uniform(jax.random.fold_in(jax.random.fold_in(rng, 6), dim), (parts,), jnp.float32, least / len(split), high / len(split))
        loudness = loudness * jnp.repeat(jnp.exp(heights), dims[dim] // parts).reshape((-1,) + (1,) * (len(dims) - 1 - dim))
    return loudness


def bell_draw(key, shape, deviation, most, split=(), kind=jnp.bfloat16):
    gain = shard_levels(key, shape, split, -0.22, 0.18) if split else 1.0
    entries = jax.random.normal(key, shape, jnp.float32) * deviation * gain
    return jnp.minimum(jnp.maximum(entries, -most), most).astype(kind)


def setup_inputs(seed: int = 0) -> dict:
    key_of = jax.random.split(jax.random.key(seed), 4)
    return {
        "forcing": bell_draw(key_of[0], (NBX, NBY, 3, NODES, NODES * NODES), 1.0, 6.0, ((0, 32), (1, 4)), jnp.float32),
        "modulus": jnp.clip(jnp.exp(math.log(4.0) - 2.0794415 * jax.random.uniform(key_of[1], (NBX, NBY, 3), jnp.float32) ** shard_levels(key_of[1], (NBX, NBY, 3), ((0, 32), (1, 4)), -0.2, 0.2)), 0.5, 4.0),
        "orient_codes": plant(jax.random.randint(key_of[2], (NBX, NBY), 0, 4), jax.random.fold_in(key_of[2], 1), 0, 3).astype(jnp.int32),
    }


mass_shift = 0.02
inject_scale = 2.0
traction_mix = 0.5
penalty_mix = 0.25
lower_edge = 0.3
upper_edge = 1.5
highest = lax.Precision.HIGHEST

def tables(extent):
    node_index = jnp.arange(extent, dtype=jnp.float32) + 1.0
    basis = math.sqrt(2.0 / (extent + 1)) * jnp.sin(math.pi * node_index[:, None] * node_index[None, :] / (extent + 1))
    eigenvalues = 2.0 - 2.0 * jnp.cos(math.pi * node_index / (extent + 1))
    return (basis, eigenvalues)

def tangent_matrix(extent):
    node_index = jnp.arange(extent, dtype=jnp.int32)
    distance = jnp.abs(node_index[:, None] - node_index[None, :])
    end_rows = ((node_index == 0) | (node_index == extent - 1)).astype(jnp.float32)
    adjacent = (distance == 1).astype(jnp.float32)
    diagonal_part = (distance == 0).astype(jnp.float32) * (2.0 - end_rows[:, None])
    return adjacent - diagonal_part

def step_weights(step_count):
    midpoint = 0.5 * (upper_edge + lower_edge)
    radius = 0.5 * (upper_edge - lower_edge)
    return [1.0 / (midpoint + radius * math.cos(math.pi * (2 * turn_index + 1) / (2 * step_count))) for turn_index in range(step_count)]

def divisor(moduli, eigenvalues):
    extent = eigenvalues.shape[0]
    summed = eigenvalues[:, None, None] + eigenvalues[None, :, None] + eigenvalues[None, None, :]
    scaled = moduli[..., None, None, None] * summed + mass_shift
    return scaled.reshape(moduli.shape + (extent, extent * extent))

def transform(source_field, basis):
    extent = basis.shape[0]
    full_shape = source_field.shape
    cube_view = source_field.reshape(full_shape[:-1] + (extent, extent))
    cube_view = jnp.einsum('ix,...xyz->...iyz', basis, cube_view, precision=highest)
    cube_view = jnp.einsum('jy,...xyz->...xjz', basis, cube_view, precision=highest)
    cube_view = jnp.einsum('kz,...xyz->...xyk', basis, cube_view, precision=highest)
    return cube_view.reshape(full_shape)

def block_solve(right_side, moduli, basis, eigenvalues):
    return transform(transform(right_side, basis) / divisor(moduli, eigenvalues), basis)

def orient(face_field, code_table, extent):
    square = face_field.reshape(face_field.shape[:-1] + (extent, extent))
    flip_rows = (code_table % 2 == 1)[..., None, None, None]
    flip_cols = (code_table // 2 == 1)[..., None, None, None]
    square = jnp.where(flip_rows, jnp.flip(square, -2), square)
    square = jnp.where(flip_cols, jnp.flip(square, -1), square)
    return square.reshape(face_field.shape)

def face_data(solution, moduli):
    extent = solution.shape[-2]
    cube_view = solution.reshape(solution.shape[:-1] + (extent, extent))
    flat_shape = solution.shape[:-2] + (extent * extent,)

    def pack_side(planes):
        normal_slope = 11.0 / 6.0 * planes[0] - 3.0 * planes[1] + 1.5 * planes[2] - planes[3] / 3.0
        return (planes[0], moduli[..., None] * normal_slope)
    x_high = pack_side([solution[..., extent - 1 - plane_depth, :] for plane_depth in range(4)])
    x_low = pack_side([solution[..., plane_depth, :] for plane_depth in range(4)])
    y_high = pack_side([cube_view[..., extent - 1 - plane_depth, :].reshape(flat_shape) for plane_depth in range(4)])
    y_low = pack_side([cube_view[..., plane_depth, :].reshape(flat_shape) for plane_depth in range(4)])
    return (x_high, x_low, y_high, y_low)

def place_faces(source_field, moduli, x_low, x_high, y_low, y_high):
    extent = source_field.shape[-2]
    added = jnp.zeros_like(source_field)
    added = added.at[..., 0, :].add(x_low)
    added = added.at[..., extent - 1, :].add(x_high)
    cube_view = added.reshape(added.shape[:-1] + (extent, extent))
    low_square = y_low.reshape(y_low.shape[:-1] + (extent, extent))
    high_square = y_high.reshape(y_high.shape[:-1] + (extent, extent))
    cube_view = cube_view.at[..., 0, :].add(low_square)
    cube_view = cube_view.at[..., extent - 1, :].add(high_square)
    added = cube_view.reshape(source_field.shape)
    return source_field + inject_scale * moduli[..., None, None] * added

def trace_update(current, side_a, side_b, moduli_a, moduli_b, omega_step, tangent):
    extent = tangent.shape[0]
    weight_a = moduli_a[..., None]
    weight_b = moduli_b[..., None]
    residue = (weight_a * side_a[0] + weight_b * side_b[0] + traction_mix * (side_a[1] + side_b[1])) / (weight_a + weight_b) - current
    rows_view = residue.reshape(residue.shape[:-1] + (residue.shape[-1] // extent, extent))
    smoothed = rows_view + penalty_mix * jnp.einsum('...z,zk->...k', rows_view, tangent, precision=highest)
    return current + omega_step * smoothed.reshape(residue.shape)

def reference(forcing, modulus, orient_codes):
    slab_count = forcing.shape[0]
    extent = forcing.shape[3]
    basis, eigenvalues = tables(extent)
    tangent = tangent_matrix(extent)
    omegas = step_weights(ITERS)
    lam_x = jnp.zeros(forcing.shape[:3] + (extent * extent,), jnp.float32)
    lam_y = jnp.zeros(forcing.shape[:3] + (extent * extent,), jnp.float32)
    live_slab = (jnp.arange(slab_count) < slab_count - 1).astype(jnp.float32)[:, None, None, None]
    codes_below = jnp.concatenate([jnp.zeros_like(orient_codes[:1]), orient_codes[:-1]], 0)
    moduli_upper = jnp.concatenate([modulus[1:], jnp.zeros_like(modulus[:1])], 0)

    def solve_pair(block_pair):
        return block_solve(block_pair[0], block_pair[1], basis, eigenvalues)
    for sweep in range(ITERS + 1):
        x_low = orient(jnp.concatenate([jnp.zeros_like(lam_x[:1]), lam_x[:-1]], 0), codes_below, extent)
        y_low = jnp.roll(lam_y, 1, axis=1)
        right_side = place_faces(forcing, modulus, x_low, lam_x, y_low, lam_y)
        flat_rhs = right_side.reshape((-1,) + forcing.shape[2:])
        solution = lax.map(solve_pair, (flat_rhs, modulus.reshape(-1, 3))).reshape(forcing.shape)
        if sweep == ITERS:
            return solution
        x_high_side, x_low_side, y_high_side, y_low_side = face_data(solution, modulus)
        upper_value = orient(jnp.concatenate([x_low_side[0][1:], jnp.zeros_like(x_low_side[0][:1])], 0), orient_codes, extent)
        upper_slope = orient(jnp.concatenate([x_low_side[1][1:], jnp.zeros_like(x_low_side[1][:1])], 0), orient_codes, extent)
        lam_x = trace_update(lam_x, x_high_side, (upper_value, upper_slope), modulus, moduli_upper, omegas[sweep], tangent) * live_slab
        beside = (jnp.roll(y_low_side[0], -1, axis=1), jnp.roll(y_low_side[1], -1, axis=1))
        lam_y = trace_update(lam_y, y_high_side, beside, modulus, jnp.roll(modulus, -1, axis=1), omegas[sweep], tangent)
    return lam_x
```

```python
import functools
import math

import jax
import jax.numpy as jnp
import ml_dtypes
import numpy as np
from jax import lax
from jax.experimental import pallas as pl
from jax.experimental.pallas import tpu as pltpu
from jax.sharding import PartitionSpec as P

N = 64
ITERS = 2
COMPS = 3
MESH = pl.DeviceIdType.MESH
F32 = jnp.float32
BF16 = jnp.bfloat16
mass_shift = 0.02
inject_scale = 2.0
traction_mix = 0.5
penalty_mix = 0.25
lower_edge = 0.3
upper_edge = 1.5


def split_np(a):
    a = np.asarray(a, np.float32)
    hi = a.astype(ml_dtypes.bfloat16)
    lo = (a - hi.astype(np.float32)).astype(ml_dtypes.bfloat16)
    return hi, lo


def rows3(a):
    hi, lo = split_np(a)
    return np.concatenate([hi, hi, lo], axis=1)


def square3(a):
    hi, lo = split_np(a)
    top = np.concatenate([hi, lo], axis=1)
    bottom = np.concatenate([hi, np.zeros_like(hi)], axis=1)
    return np.concatenate([top, bottom], axis=0)


def constants():
    n = np.arange(1, N + 1, dtype=np.float64)
    q = math.sqrt(2.0 / (N + 1)) * np.sin(math.pi * n[:, None] * n[None, :] / (N + 1))
    e = 2.0 - 2.0 * np.cos(math.pi * n / (N + 1))
    tangent = np.diag(np.full(N, -2.0)) + np.diag(np.ones(N - 1), 1) + np.diag(np.ones(N - 1), -1)
    tangent[0, 0] = tangent[-1, -1] = -1.0
    smooth = np.eye(N) + penalty_mix * (q @ tangent @ q)
    half = N // 2
    sign = (-1.0) ** np.arange(half)
    fold = np.block([[q, q], [q, -q]])
    even, odd = q[0::2, :half], q[1::2, :half] * sign[None, :]
    lx = rows3(q)
    ly = rows3(np.concatenate([even, odd], axis=0))
    lyi = rows3(np.concatenate([even.T, odd.T], axis=0))
    wz = square3(fold)
    mx = square3(np.kron(np.eye(2), smooth))
    normal = q[0] + traction_mix * (11.0 / 6.0 * q[0] - 3.0 * q[1] + 1.5 * q[2] - q[3] / 3.0)
    table = np.stack([normal, q[0], e]).astype(np.float32)
    spread = lambda v: np.repeat(v.reshape(half, 2), N, axis=1)
    planes = np.stack(
        [spread(normal), spread(q[0]), spread(e) + np.tile(e, 2)[None, :]]
    ).astype(np.float32)
    return lx, ly, lyi, wz, mx, table, planes


def step_weights():
    mid = 0.5 * (upper_edge + lower_edge)
    radius = 0.5 * (upper_edge - lower_edge)
    return [
        1.0 / (mid + radius * math.cos(math.pi * (2 * k + 1) / (2 * ITERS))) for k in range(ITERS)
    ]


def lane_iota():
    return lax.broadcasted_iota(jnp.int32, (1, 128), 1)


def split(a):
    hi = a.astype(BF16)
    lo = (a - hi.astype(F32)).astype(BF16)
    return hi, lo


def stack3(a):
    hi, lo = split(a)
    return jnp.concatenate([hi, lo, hi], axis=0)


def times_square(a, w):
    hi, lo = split(a)
    r = jnp.dot(jnp.concatenate([hi, lo], axis=1), w, preferred_element_type=F32)
    return r[:, :128] + r[:, 128:]


def dot(a, b):
    return jnp.dot(a, b, preferred_element_type=F32)


def forward_zx(x_ref, t_ref, wz, lx, unroll):
    low = lane_iota() < N

    def body(p, carry):
        a = x_ref[:, pl.ds(pl.multiple_of(p * 128, 128), 128)]
        b = x_ref[:, pl.ds(pl.multiple_of((31 - p) * 128, 128), 128)]
        both = jnp.concatenate([jnp.where(low, a, b), jnp.where(low, b, a)], axis=0)
        z = times_square(both, wz)
        r = dot(lx, stack3(jnp.concatenate([z[:N], z[N:]], axis=1)))
        at = pl.multiple_of(p * 128, 128)
        t_ref[pl.ds(at, N), :] = r[:, :128]
        t_ref[pl.ds(at + N, N), :] = r[:, 128:]
        return carry

    lax.fori_loop(0, 16, body, 0, unroll=unroll)


def pair_y(ly, a, b):
    low = lane_iota() < N
    r = dot(ly, stack3(jnp.concatenate([a, b], axis=1)))
    return (
        jnp.where(low, r[:32, :128], r[32:, :128]),
        jnp.where(low, r[:32, 128:], r[32:, 128:]),
    )


def orient_row(code):
    lane = lane_iota()
    rows = jnp.where(lane < N, 1.0, -1.0)
    cols = jnp.where(lane % 2 == 0, 1.0, -1.0)
    one = jnp.ones((1, 128), F32)
    return jnp.where(code % 2 == 1, rows, one) * jnp.where(code // 2 == 1, cols, one)


def face_sums(se, so, y, m, g_ref, add):
    low = lane_iota() < N
    swapped = pltpu.roll(y, N, 1)
    total, diff = y + swapped, y - swapped
    parts = [
        se - so,
        se + so,
        jnp.where(low, diff[:32], -diff[32:]),
        jnp.where(low, total[:32], total[32:]),
    ]
    for at, part in enumerate(parts):
        rows = slice(32 * at, 32 * at + 32)
        value = m * part
        g_ref[rows, :] = value + g_ref[rows, :] if add else value


def spread_traces(lam, m, lx_ref, ly_ref):
    low = lane_iota() < N
    scale = inject_scale * m
    xh, xl, yh, yl = (lam[32 * i : 32 * i + 32] for i in range(4))
    lx_ref[0] = scale * (xl + xh)
    lx_ref[1] = scale * (xl - xh)
    pe, po = scale * (yl + yh), scale * (yl - yh)
    ly_ref[0:32, :] = jnp.where(low, pe, pltpu.roll(po, N, 1))
    ly_ref[32:64, :] = jnp.where(low, pltpu.roll(pe, N, 1), po)


def trace_kernel(
    f_hbm, mod, codes, table, lx_c, ly_c, wz_c, mx_c, planes,
    u_out, g_out, tx_out, ty_out,
    xin, t_scr, y_scr, face, lam, msend, mrecv, send, recv,
    in_sem, msend_sem, mrecv_sem, send_sem, recv_sem,
):
    s, j = lax.axis_index("blk"), lax.axis_index("face")
    ns, nj = lax.axis_size("blk"), lax.axis_size("face")
    partner = [
        (lax.rem(s + ns - 1, ns), j),
        (lax.rem(s + 1, ns), j),
        (s, lax.rem(j + nj - 1, nj)),
        (s, lax.rem(j + 1, nj)),
    ]
    barrier = pltpu.get_barrier_semaphore()
    loads = [pltpu.make_async_copy(f_hbm.at[c], xin.at[c], in_sem.at[c]) for c in range(COMPS)]
    for load in loads:
        load.start()
    for device in partner:
        pl.semaphore_signal(barrier, inc=1, device_id=device, device_id_type=MESH)

    row = lax.broadcasted_iota(jnp.int32, (8, 128), 0)
    moduli = [mod[0, 0, c] for c in range(COMPS)]
    msend[...] = jnp.where(row == 0, moduli[0], jnp.where(row == 1, moduli[1], moduli[2]))
    flip = orient_row(codes[0, 0])
    live_high = jnp.where(s < ns - 1, 1.0, 0.0).astype(F32)
    live_low = jnp.where(s > 0, 1.0, 0.0).astype(F32)
    omegas = step_weights()

    def fill(i, carry):
        ejk = planes[2]
        for c in range(COMPS):
            d = moduli[c] * (ejk + table[2, i]) + mass_shift
            r = pl.reciprocal(d, approx=True)
            g_out[c, i] = r * (2.0 - d * r)
        return carry

    lax.fori_loop(0, N, fill, 0, unroll=2)

    pl.semaphore_wait(barrier, 4)

    def mcopy(d):
        return pltpu.make_async_remote_copy(
            src_ref=msend, dst_ref=mrecv.at[d], send_sem=msend_sem.at[d],
            recv_sem=mrecv_sem.at[d], device_id=partner[d], device_id_type=MESH,
        )

    def gcopy(k, c, d):
        return pltpu.make_async_remote_copy(
            src_ref=send.at[k, c, d], dst_ref=recv.at[k, c, d], send_sem=send_sem.at[k, c, d],
            recv_sem=recv_sem.at[k, c, d], device_id=partner[d], device_id_type=MESH,
        )

    for d in range(4):
        mcopy(d).start()

    def send_faces(k, c):
        send[k, c, 0] = face[c, 32:64, :]
        send[k, c, 1] = face[c, 0:32, :] * flip
        send[k, c, 2] = face[c, 96:128, :]
        send[k, c, 3] = face[c, 64:96, :]
        for d in range(4):
            gcopy(k, c, d).start()

    def reduce_group(values, base, carry):
        se, so = carry
        cj = planes[0]
        sums = []
        for n, u in enumerate(values):
            weighted = table[0, base + n] * u
            if n % 2 == 0:
                se = se + weighted
            else:
                so = so + weighted
            w = cj * u
            sums.append((w[0:8] + w[8:16]) + (w[16:24] + w[24:32]))
        y = jnp.sum(jnp.stack(sums, axis=0), axis=1)
        y_scr[pl.ds(pl.multiple_of(base, 8), 8), :] = y
        return se, so

    zero = jnp.zeros((32, 128), F32)

    for c in range(COMPS):
        loads[c].wait()
        forward_zx(xin.at[c], t_scr, wz_c[...], lx_c[...], 2)

        def solve_group(group, carry, c=c):
            base = group * 8
            values = []
            for n in range(0, 8, 2):
                a = t_scr[pl.ds(base + n, 32, stride=N), :]
                b = t_scr[pl.ds(base + n + 1, 32, stride=N), :]
                for off, h in enumerate(pair_y(ly_c[...], a, b)):
                    u = h * g_out[c, base + n + off]
                    u_out[c, base + n + off] = u
                    values.append(u)
            return reduce_group(values, base, carry)

        se, so = lax.fori_loop(0, 8, solve_group, (zero, zero))
        face_sums(se, so, y_scr[...], moduli[c], face.at[c], False)
        send_faces(0, c)

    for d in range(4):
        mcopy(d).wait_recv()

    def update(k, c):
        for d in range(4):
            gcopy(k, c, d).wait_recv()
        m = moduli[c]
        order = [0, 1, 2, 3]
        residues = []
        for at, d in enumerate(order):
            other = recv[k, c, d]
            if d == 0:
                other = other * flip
            inverse = 1.0 / (m + mrecv[d, c : c + 1, :])
            r = (face[c, 32 * at : 32 * at + 32, :] + other) * inverse
            if k > 0:
                r = r - lam[c, 32 * at : 32 * at + 32, :]
            if d == 0:
                r = r * live_high
            if d == 1:
                r = r * live_low
            residues.append(r)
        step = omegas[k] * times_square(jnp.concatenate(residues, axis=0), mx_c[...])
        new = step + lam[c] if k > 0 else step
        lam[c] = new
        spread_traces(new, m, tx_out.at[c], ty_out.at[c])

    for c in range(COMPS):
        update(0, c)

        def move_group(group, carry, c=c):
            base = group * 8
            values = []
            q0j = planes[1]
            for n in range(8):
                i = base + n
                add = table[1, i] * tx_out[c, n % 2] + q0j * ty_out[c, pl.ds(i, 1), :]
                values.append(g_out[c, i] * add)
            return reduce_group(values, base, carry)

        se, so = lax.fori_loop(0, 8, move_group, (zero, zero))
        face_sums(se, so, y_scr[...], moduli[c], face.at[c], True)
        send_faces(1, c)

    for c in range(COMPS):
        update(1, c)
    for d in range(4):
        mcopy(d).wait_send()
    for k in range(ITERS):
        for c in range(COMPS):
            for d in range(4):
                gcopy(k, c, d).wait_send()


CHUNKS = 4


def back_kernel(u_ref, g_ref, tx, ty, table, lx_c, lyi_c, wz_c, planes, out_hbm, t_scr, o_scr, out_sem):
    low = lane_iota() < N

    def ocopy(c, chunk, side):
        first = chunk * 512 if side == 0 else 3584 - chunk * 512
        return pltpu.make_async_copy(
            o_scr.at[c, :, pl.ds(first, 512)],
            out_hbm.at[c, :, pl.ds(first, 512)],
            out_sem.at[c, chunk, side],
        )

    for c in range(COMPS):

        def solve_pair(pair, carry, c=c):
            q0j = planes[1]
            values = []
            for n in range(2):
                i = pair * 2 + n
                add = table[1, i] * tx[c, n] + q0j * ty[c, pl.ds(i, 1), :]
                values.append(u_ref[c, i] + g_ref[c, i] * add)
            a, b = pair_y(lyi_c[...], *values)
            t_scr[pl.ds(pair * 2, 32, stride=N), :] = a
            t_scr[pl.ds(pair * 2 + 1, 32, stride=N), :] = b
            return carry

        lax.fori_loop(0, 32, solve_pair, 0, unroll=4)

        def body(p, carry, c=c):
            at = pl.multiple_of(p * 128, 128)
            z = jnp.concatenate([t_scr[pl.ds(at, N), :], t_scr[pl.ds(at + N, N), :]], axis=1)
            r = dot(lx_c[...], stack3(z))
            o = times_square(jnp.concatenate([r[:, :128], r[:, 128:]], axis=0), wz_c[...])
            a, b = o[:N], o[N:]
            o_scr[c, :, pl.ds(at, 128)] = jnp.where(low, a, b)
            o_scr[c, :, pl.ds(pl.multiple_of((31 - p) * 128, 128), 128)] = jnp.where(low, b, a)
            return carry

        for chunk in range(CHUNKS):
            lax.fori_loop(4 * chunk, 4 * chunk + 4, body, 0, unroll=2)
            ocopy(c, chunk, 0).start()
            ocopy(c, chunk, 1).start()
    for c in range(COMPS):
        for chunk in range(CHUNKS):
            ocopy(c, chunk, 0).wait()
            ocopy(c, chunk, 1).wait()


def shards(forcing, modulus, orient_codes):
    lx, ly, lyi, wz, mx, table, planes = (jnp.asarray(a) for a in constants())
    f = forcing.reshape(COMPS, N, N * N)
    vmem = pl.BlockSpec(memory_space=pltpu.VMEM)
    smem = pl.BlockSpec(memory_space=pltpu.SMEM)
    hbm = pl.BlockSpec(memory_space=pltpu.HBM)
    spectral = (COMPS, N, N // 2, 128)
    shapes = [spectral, spectral, (COMPS, 2, 32, 128), (COMPS, N, 128)]
    u, g, tx, ty = pl.pallas_call(
        trace_kernel,
        out_shape=[pltpu.VMEM(shape, F32) for shape in shapes],
        in_specs=[hbm, smem, smem, smem, vmem, vmem, vmem, vmem, vmem],
        out_specs=[vmem] * 4,
        scratch_shapes=[
            pltpu.VMEM((COMPS, N, N * N), F32),
            pltpu.VMEM((32 * N, 128), F32),
            pltpu.VMEM((N, 128), F32),
            pltpu.VMEM((COMPS, 128, 128), F32),
            pltpu.VMEM((COMPS, 128, 128), F32),
            pltpu.VMEM((8, 128), F32),
            pltpu.VMEM((4, 8, 128), F32),
            pltpu.VMEM((ITERS, COMPS, 4, 32, 128), F32),
            pltpu.VMEM((ITERS, COMPS, 4, 32, 128), F32),
            pltpu.SemaphoreType.DMA((COMPS,)),
            pltpu.SemaphoreType.DMA((4,)),
            pltpu.SemaphoreType.DMA((4,)),
            pltpu.SemaphoreType.DMA((ITERS, COMPS, 4)),
            pltpu.SemaphoreType.DMA((ITERS, COMPS, 4)),
        ],
        compiler_params=pltpu.CompilerParams(
            collective_id=0, has_side_effects=True, vmem_limit_bytes=40 * 2**20
        ),
        cost_estimate=pl.CostEstimate(flops=2 * 10**9, bytes_accessed=3 * 2**20, transcendentals=0),
        name="traces",
    )(f, modulus, orient_codes, table, lx, ly, wz, mx, planes)
    out = pl.pallas_call(
        back_kernel,
        out_shape=jax.ShapeDtypeStruct((COMPS, N, N * N), F32),
        in_specs=[vmem] * 4 + [smem] + [vmem] * 4,
        out_specs=hbm,
        scratch_shapes=[
            pltpu.VMEM((32 * N, 128), F32),
            pltpu.VMEM((COMPS, N, N * N), F32),
            pltpu.SemaphoreType.DMA((COMPS, CHUNKS, 2)),
        ],
        compiler_params=pltpu.CompilerParams(vmem_limit_bytes=40 * 2**20),
        cost_estimate=pl.CostEstimate(flops=2 * 10**9, bytes_accessed=3 * 2**20, transcendentals=0),
        name="back",
    )(u, g, tx, ty, table, lx, lyi, wz, planes)
    return out.reshape(forcing.shape)


def solution(mesh):
    placed = (P("blk", "face", None, None, None), P("blk", "face", None), P("blk", "face"))
    return jax.shard_map(
        shards,
        mesh=mesh,
        in_specs=placed,
        out_specs=P("blk", "face", None, None, None),
        check_vma=False,
    )
```

```python
import functools
import math

import jax
import jax.numpy as jnp
import ml_dtypes
import numpy as np
from jax import lax
from jax.experimental import pallas as pl
from jax.experimental.pallas import tpu as pltpu
from jax.sharding import PartitionSpec as P

N = 64
ITERS = 2
COMPS = 3
STRIDE = 72
MESH = pl.DeviceIdType.MESH
F32 = jnp.float32
BF16 = jnp.bfloat16
mass_shift = 0.02
inject_scale = 2.0
traction_mix = 0.5
penalty_mix = 0.25
lower_edge = 0.3
upper_edge = 1.5


def in_hbm(a):
    return pltpu.with_memory_space_constraint(a, pltpu.HBM)


def split_np(a):
    a = np.asarray(a, np.float32)
    hi = a.astype(ml_dtypes.bfloat16)
    lo = (a - hi.astype(np.float32)).astype(ml_dtypes.bfloat16)
    return hi, lo


def rows3(a):
    hi, lo = split_np(a)
    return np.concatenate([hi, hi, lo], axis=1)


def square3(a):
    hi, lo = split_np(a)
    top = np.concatenate([hi, lo], axis=1)
    bottom = np.concatenate([hi, np.zeros_like(hi)], axis=1)
    return np.concatenate([top, bottom], axis=0)


def constants():
    n = np.arange(1, N + 1, dtype=np.float64)
    q = math.sqrt(2.0 / (N + 1)) * np.sin(math.pi * n[:, None] * n[None, :] / (N + 1))
    e = 2.0 - 2.0 * np.cos(math.pi * n / (N + 1))
    tangent = np.diag(np.full(N, -2.0)) + np.diag(np.ones(N - 1), 1) + np.diag(np.ones(N - 1), -1)
    tangent[0, 0] = tangent[-1, -1] = -1.0
    smooth = np.eye(N) + penalty_mix * (q @ tangent @ q)
    half = N // 2
    sign = (-1.0) ** np.arange(half)
    fold = np.block([[q, q], [q, -q]])
    even, odd = q[0::2, :half], q[1::2, :half] * sign[None, :]
    lx = rows3(q)
    ly = rows3(np.concatenate([even, odd], axis=0))
    lyi = rows3(np.concatenate([even.T, odd.T], axis=0))
    wz = square3(fold)
    mx = square3(np.kron(np.eye(2), smooth))
    normal = q[0] + traction_mix * (11.0 / 6.0 * q[0] - 3.0 * q[1] + 1.5 * q[2] - q[3] / 3.0)
    table = np.stack([normal, q[0], e]).astype(np.float32)
    spread = lambda v: np.repeat(v.reshape(half, 2), N, axis=1)
    planes = np.stack(
        [spread(normal), spread(q[0]), spread(e) + np.tile(e, 2)[None, :]]
    ).astype(np.float32)
    return lx, ly, lyi, wz, mx, table, planes


def step_weights():
    mid = 0.5 * (upper_edge + lower_edge)
    radius = 0.5 * (upper_edge - lower_edge)
    return [
        1.0 / (mid + radius * math.cos(math.pi * (2 * k + 1) / (2 * ITERS))) for k in range(ITERS)
    ]


def lane_iota():
    return lax.broadcasted_iota(jnp.int32, (1, 128), 1)


def split(a):
    hi = a.astype(BF16)
    lo = (a - hi.astype(F32)).astype(BF16)
    return hi, lo


def stack3(a):
    hi, lo = split(a)
    return jnp.concatenate([hi, lo, hi], axis=0)


def times_square(a, w):
    hi, lo = split(a)
    r = jnp.dot(jnp.concatenate([hi, lo], axis=1), w, preferred_element_type=F32)
    return r[:, :128] + r[:, 128:]


def dot(a, b):
    return jnp.dot(a, b, preferred_element_type=F32)


def row_at(y):
    return slice(y * STRIDE, y * STRIDE + N)


def z_forward(x_ref, t_ref, wz):
    low = lane_iota() < N
    for p in range(16):
        a = x_ref[:, p * 128 : p * 128 + 128]
        b = x_ref[:, (31 - p) * 128 : (32 - p) * 128]
        z = times_square(jnp.concatenate([jnp.where(low, a, b), jnp.where(low, b, a)], axis=0), wz)
        t_ref[row_at(2 * p), :] = z[:N]
        t_ref[row_at(2 * p + 1), :] = z[N:]


def x_either(a_ref, b_ref, lx):
    for p in range(16):
        a = jnp.concatenate([a_ref[row_at(2 * p), :], a_ref[row_at(2 * p + 1), :]], axis=1)
        r = dot(lx, stack3(a))
        b_ref[row_at(2 * p), :] = r[:, :128]
        b_ref[row_at(2 * p + 1), :] = r[:, 128:]


def z_back(t_ref, o_ref, wz, p):
    low = lane_iota() < N
    both = jnp.concatenate([t_ref[row_at(2 * p), :], t_ref[row_at(2 * p + 1), :]], axis=0)
    o = times_square(both, wz)
    a, b = o[:N], o[N:]
    o_ref[:, p * 128 : p * 128 + 128] = jnp.where(low, a, b)
    o_ref[:, (31 - p) * 128 : (32 - p) * 128] = jnp.where(low, b, a)


def pair_y(ly, a, b):
    low = lane_iota() < N
    r = dot(ly, stack3(jnp.concatenate([a, b], axis=1)))
    return (
        jnp.where(low, r[:32, :128], r[32:, :128]),
        jnp.where(low, r[:32, 128:], r[32:, 128:]),
    )


def orient_row(code):
    lane = lane_iota()
    rows = jnp.where(lane < N, 1.0, -1.0)
    cols = jnp.where(lane % 2 == 0, 1.0, -1.0)
    one = jnp.ones((1, 128), F32)
    return jnp.where(code % 2 == 1, rows, one) * jnp.where(code // 2 == 1, cols, one)


def face_sums(se, so, y, m, g_ref, add):
    low = lane_iota() < N
    swapped = pltpu.roll(y, N, 1)
    total, diff = y + swapped, y - swapped
    parts = [
        se - so,
        se + so,
        jnp.where(low, diff[:32], -diff[32:]),
        jnp.where(low, total[:32], total[32:]),
    ]
    for at, part in enumerate(parts):
        rows = slice(32 * at, 32 * at + 32)
        value = m * part
        g_ref[rows, :] = value + g_ref[rows, :] if add else value


def spread_traces(lam, m, lx_ref, ly_ref):
    low = lane_iota() < N
    scale = inject_scale * m
    xh, xl, yh, yl = (lam[32 * i : 32 * i + 32] for i in range(4))
    lx_ref[0] = scale * (xl + xh)
    lx_ref[1] = scale * (xl - xh)
    pe, po = scale * (yl + yh), scale * (yl - yh)
    ly_ref[0:32, :] = jnp.where(low, pe, pltpu.roll(po, N, 1))
    ly_ref[32:64, :] = jnp.where(low, pltpu.roll(pe, N, 1), po)


def trace_kernel(
    f_hbm, mod_h, codes, table_h, lx_h, ly_h, wz_h, mx_h, planes_h,
    u_out, g_out, tx_out, ty_out,
    mod, table, lx_c, ly_c, wz_c, mx_c, planes, xin, t_scr, x_scr, y_scr, face, lam, msend, mrecv, send, recv,
    in_sem, con_sem, msend_sem, mrecv_sem, send_sem, recv_sem,
):
    s, j = lax.axis_index("blk"), lax.axis_index("face")
    ns, nj = lax.axis_size("blk"), lax.axis_size("face")
    partner = [
        (lax.rem(s + ns - 1, ns), j),
        (lax.rem(s + 1, ns), j),
        (s, lax.rem(j + nj - 1, nj)),
        (s, lax.rem(j + 1, nj)),
    ]
    barrier = pltpu.get_barrier_semaphore()
    loads = [pltpu.make_async_copy(f_hbm.at[c], xin.at[c], in_sem.at[c]) for c in range(COMPS)]
    pairs = [
        (mod_h, mod), (table_h, table), (planes_h, planes),
        (wz_h, wz_c), (lx_h, lx_c), (ly_h, ly_c), (mx_h, mx_c),
    ]
    small = [pltpu.make_async_copy(a, b, con_sem.at[i]) for i, (a, b) in enumerate(pairs)]
    for copy in small[:3]:
        copy.start()
    loads[0].start()
    for copy in small[3:]:
        copy.start()
    for load in loads[1:]:
        load.start()
    for device in partner:
        pl.semaphore_signal(barrier, inc=1, device_id=device, device_id_type=MESH)

    for copy in small[:3]:
        copy.wait()
    row = lax.broadcasted_iota(jnp.int32, (8, 128), 0)
    moduli = [mod[0, 0, c] for c in range(COMPS)]
    msend[...] = jnp.where(row == 0, moduli[0], jnp.where(row == 1, moduli[1], moduli[2]))
    flip = orient_row(codes[0, 0])
    live_high = jnp.where(s < ns - 1, 1.0, 0.0).astype(F32)
    live_low = jnp.where(s > 0, 1.0, 0.0).astype(F32)
    omegas = step_weights()

    def fill(i, carry):
        ejk = planes[2]
        for c in range(COMPS):
            d = moduli[c] * (ejk + table[2, i]) + mass_shift
            r = pl.reciprocal(d, approx=True)
            g_out[c, i] = r * (2.0 - d * r)
        return carry

    lax.fori_loop(0, N, fill, 0, unroll=4)

    pl.semaphore_wait(barrier, 4)

    def mcopy(d):
        return pltpu.make_async_remote_copy(
            src_ref=msend, dst_ref=mrecv.at[d], send_sem=msend_sem.at[d],
            recv_sem=mrecv_sem.at[d], device_id=partner[d], device_id_type=MESH,
        )

    def gcopy(k, c, d):
        return pltpu.make_async_remote_copy(
            src_ref=send.at[k, c, d], dst_ref=recv.at[k, c, d], send_sem=send_sem.at[k, c, d],
            recv_sem=recv_sem.at[k, c, d], device_id=partner[d], device_id_type=MESH,
        )

    for d in range(4):
        mcopy(d).start()
    for copy in small[3:]:
        copy.wait()

    def send_faces(k, c):
        send[k, c, 0] = face[c, 32:64, :]
        send[k, c, 1] = face[c, 0:32, :] * flip
        send[k, c, 2] = face[c, 96:128, :]
        send[k, c, 3] = face[c, 64:96, :]
        for d in range(4):
            gcopy(k, c, d).start()

    def reduce_group(values, base, carry):
        se, so = carry
        cj = planes[0]
        sums = []
        for n, u in enumerate(values):
            weighted = table[0, base + n] * u
            if n % 2 == 0:
                se = se + weighted
            else:
                so = so + weighted
            w = cj * u
            sums.append((w[0:8] + w[8:16]) + (w[16:24] + w[24:32]))
        y = jnp.sum(jnp.stack(sums, axis=0), axis=1)
        y_scr[base : base + 8, :] = y
        return se, so

    zero = jnp.zeros((32, 128), F32)

    def forward(c):
        loads[c].wait()
        z_forward(xin.at[c], t_scr, wz_c[...])
        x_either(t_scr, x_scr, lx_c[...])
        sums = (zero, zero)
        for base in range(0, N, 8):
            values = []
            for n in range(0, 8, 2):
                a = x_scr[pl.ds(base + n, 32, stride=STRIDE), :]
                b = x_scr[pl.ds(base + n + 1, 32, stride=STRIDE), :]
                for off, h in enumerate(pair_y(ly_c[...], a, b)):
                    u = h * g_out[c, base + n + off]
                    u_out[c, base + n + off] = u
                    values.append(u)
            sums = reduce_group(values, base, sums)
        face_sums(*sums, y_scr[...], moduli[c], face.at[c], False)
        send_faces(0, c)

    def update(k, c):
        for d in range(4):
            gcopy(k, c, d).wait_recv()
        m = moduli[c]
        order = [0, 1, 2, 3]
        residues = []
        for at, d in enumerate(order):
            other = recv[k, c, d]
            if d == 0:
                other = other * flip
            inverse = 1.0 / (m + mrecv[d, c : c + 1, :])
            r = (face[c, 32 * at : 32 * at + 32, :] + other) * inverse
            if k > 0:
                r = r - lam[c, 32 * at : 32 * at + 32, :]
            if d == 0:
                r = r * live_high
            if d == 1:
                r = r * live_low
            residues.append(r)
        step = omegas[k] * times_square(jnp.concatenate(residues, axis=0), mx_c[...])
        new = step + lam[c] if k > 0 else step
        lam[c] = new
        spread_traces(new, m, tx_out.at[c], ty_out.at[c])

    def move(c):
        update(0, c)
        sums = (zero, zero)
        q0j = planes[1]
        for base in range(0, N, 8):
            values = []
            for i in range(base, base + 8):
                add = table[1, i] * tx_out[c, i % 2] + q0j * ty_out[c, i : i + 1, :]
                values.append(g_out[c, i] * add)
            sums = reduce_group(values, base, sums)
        face_sums(*sums, y_scr[...], moduli[c], face.at[c], True)
        send_faces(1, c)

    forward(0)
    forward(1)
    for d in range(4):
        mcopy(d).wait_recv()
    move(0)
    forward(2)
    move(1)
    move(2)
    for c in range(COMPS):
        update(1, c)
    for d in range(4):
        mcopy(d).wait_send()
    for k in range(ITERS):
        for c in range(COMPS):
            for d in range(4):
                gcopy(k, c, d).wait_send()


CHUNKS = 4


def back_kernel(u_ref, g_ref, tx, ty, table, lx_c, lyi_c, wz_c, planes, out_hbm, t_scr, x_scr, o_scr, out_sem):

    def ocopy(c, chunk, side):
        first = chunk * 512 if side == 0 else 3584 - chunk * 512
        return pltpu.make_async_copy(
            o_scr.at[c, :, pl.ds(first, 512)],
            out_hbm.at[c, :, pl.ds(first, 512)],
            out_sem.at[c, chunk, side],
        )

    for c in range(COMPS):
        q0j = planes[1]
        for i in range(0, N, 2):
            values = []
            for n in range(2):
                add = table[1, i + n] * tx[c, n] + q0j * ty[c, i + n : i + n + 1, :]
                values.append(u_ref[c, i + n] + g_ref[c, i + n] * add)
            a, b = pair_y(lyi_c[...], *values)
            t_scr[pl.ds(i, 32, stride=STRIDE), :] = a
            t_scr[pl.ds(i + 1, 32, stride=STRIDE), :] = b
        x_either(t_scr, x_scr, lx_c[...])
        for chunk in range(CHUNKS):
            for p in range(4 * chunk, 4 * chunk + 4):
                z_back(x_scr, o_scr.at[c], wz_c[...], p)
            ocopy(c, chunk, 0).start()
            ocopy(c, chunk, 1).start()
    for c in range(COMPS):
        for chunk in range(CHUNKS):
            ocopy(c, chunk, 0).wait()
            ocopy(c, chunk, 1).wait()


def shards(forcing, modulus, orient_codes):
    lx, ly, lyi, wz, mx, table, planes = (jnp.asarray(a) for a in constants())
    f = forcing.reshape(COMPS, N, N * N)
    vmem = pl.BlockSpec(memory_space=pltpu.VMEM)
    smem = pl.BlockSpec(memory_space=pltpu.SMEM)
    hbm = pl.BlockSpec(memory_space=pltpu.HBM)
    spectral = (COMPS, N, N // 2, 128)
    shapes = [spectral, spectral, (COMPS, 2, 32, 128), (COMPS, N, 128)]
    u, g, tx, ty = pl.pallas_call(
        trace_kernel,
        out_shape=[pltpu.VMEM(shape, F32) for shape in shapes],
        in_specs=[hbm, hbm, smem] + [hbm] * 6,
        out_specs=[vmem] * 4,
        scratch_shapes=[
            pltpu.SMEM((1, 1, COMPS), F32),
            pltpu.SMEM(table.shape, F32),
            pltpu.VMEM(lx.shape, BF16),
            pltpu.VMEM(ly.shape, BF16),
            pltpu.VMEM(wz.shape, BF16),
            pltpu.VMEM(mx.shape, BF16),
            pltpu.VMEM(planes.shape, F32),
            pltpu.VMEM((COMPS, N, N * N), F32),
            pltpu.VMEM((32 * STRIDE, 128), F32),
            pltpu.VMEM((32 * STRIDE, 128), F32),
            pltpu.VMEM((N, 128), F32),
            pltpu.VMEM((COMPS, 128, 128), F32),
            pltpu.VMEM((COMPS, 128, 128), F32),
            pltpu.VMEM((8, 128), F32),
            pltpu.VMEM((4, 8, 128), F32),
            pltpu.VMEM((ITERS, COMPS, 4, 32, 128), F32),
            pltpu.VMEM((ITERS, COMPS, 4, 32, 128), F32),
            pltpu.SemaphoreType.DMA((COMPS,)),
            pltpu.SemaphoreType.DMA((7,)),
            pltpu.SemaphoreType.DMA((4,)),
            pltpu.SemaphoreType.DMA((4,)),
            pltpu.SemaphoreType.DMA((ITERS, COMPS, 4)),
            pltpu.SemaphoreType.DMA((ITERS, COMPS, 4)),
        ],
        compiler_params=pltpu.CompilerParams(
            collective_id=0, has_side_effects=True, vmem_limit_bytes=40 * 2**20
        ),
        cost_estimate=pl.CostEstimate(flops=2 * 10**9, bytes_accessed=3 * 2**20, transcendentals=0),
        name="traces",
    )(in_hbm(f), in_hbm(modulus), orient_codes, *(in_hbm(a) for a in (table, lx, ly, wz, mx, planes)))
    out = pl.pallas_call(
        back_kernel,
        out_shape=jax.ShapeDtypeStruct((COMPS, N, N * N), F32),
        in_specs=[vmem] * 4 + [smem] + [vmem] * 4,
        out_specs=hbm,
        scratch_shapes=[
            pltpu.VMEM((32 * STRIDE, 128), F32),
            pltpu.VMEM((32 * STRIDE, 128), F32),
            pltpu.VMEM((COMPS, N, N * N), F32),
            pltpu.SemaphoreType.DMA((COMPS, CHUNKS, 2)),
        ],
        compiler_params=pltpu.CompilerParams(vmem_limit_bytes=40 * 2**20),
        cost_estimate=pl.CostEstimate(flops=2 * 10**9, bytes_accessed=3 * 2**20, transcendentals=0),
        name="back",
    )(u, g, tx, ty, table, lx, lyi, wz, planes)
    return out.reshape(forcing.shape)


def solution(mesh):
    placed = (P("blk", "face", None, None, None), P("blk", "face", None), P("blk", "face"))
    return jax.shard_map(
        shards,
        mesh=mesh,
        in_specs=placed,
        out_specs=P("blk", "face", None, None, None),
        check_vma=False,
    )
```

```python
import functools
import math

import jax
import jax.numpy as jnp
import ml_dtypes
import numpy as np
from jax import lax
from jax.experimental import pallas as pl
from jax.experimental.pallas import tpu as pltpu
from jax.sharding import PartitionSpec as P

N = 64
ITERS = 2
COMPS = 3
STRIDE = 72
MESH = pl.DeviceIdType.MESH
F32 = jnp.float32
BF16 = jnp.bfloat16
mass_shift = 0.02
inject_scale = 2.0
traction_mix = 0.5
penalty_mix = 0.25
lower_edge = 0.3
upper_edge = 1.5


def in_hbm(a):
    return pltpu.with_memory_space_constraint(a, pltpu.HBM)


def split_np(a):
    a = np.asarray(a, np.float32)
    hi = a.astype(ml_dtypes.bfloat16)
    lo = (a - hi.astype(np.float32)).astype(ml_dtypes.bfloat16)
    return hi, lo


def rows3(a):
    hi, lo = split_np(a)
    return np.concatenate([hi, hi, lo], axis=1)


def square3(a):
    hi, lo = split_np(a)
    top = np.concatenate([hi, lo], axis=1)
    bottom = np.concatenate([hi, np.zeros_like(hi)], axis=1)
    return np.concatenate([top, bottom], axis=0)


def constants():
    n = np.arange(1, N + 1, dtype=np.float64)
    q = math.sqrt(2.0 / (N + 1)) * np.sin(math.pi * n[:, None] * n[None, :] / (N + 1))
    e = 2.0 - 2.0 * np.cos(math.pi * n / (N + 1))
    tangent = np.diag(np.full(N, -2.0)) + np.diag(np.ones(N - 1), 1) + np.diag(np.ones(N - 1), -1)
    tangent[0, 0] = tangent[-1, -1] = -1.0
    smooth = np.eye(N) + penalty_mix * (q @ tangent @ q)
    half = N // 2
    sign = (-1.0) ** np.arange(half)
    fold = np.block([[q, q], [q, -q]])
    even, odd = q[0::2, :half], q[1::2, :half] * sign[None, :]
    lx = rows3(q)
    ly = rows3(np.concatenate([even, odd], axis=0))
    lyi = rows3(np.concatenate([even.T, odd.T], axis=0))
    wz = square3(fold)
    mx = square3(np.kron(np.eye(2), smooth))
    normal = q[0] + traction_mix * (11.0 / 6.0 * q[0] - 3.0 * q[1] + 1.5 * q[2] - q[3] / 3.0)
    table = np.stack([normal, q[0], e]).astype(np.float32)
    spread = lambda v: np.repeat(v.reshape(half, 2), N, axis=1)
    planes = np.stack(
        [spread(normal), spread(q[0]), spread(e) + np.tile(e, 2)[None, :]]
    ).astype(np.float32)
    return lx, ly, lyi, wz, mx, table, planes


def step_weights():
    mid = 0.5 * (upper_edge + lower_edge)
    radius = 0.5 * (upper_edge - lower_edge)
    return [
        1.0 / (mid + radius * math.cos(math.pi * (2 * k + 1) / (2 * ITERS))) for k in range(ITERS)
    ]


def lane_iota():
    return lax.broadcasted_iota(jnp.int32, (1, 128), 1)


def split(a):
    hi = a.astype(BF16)
    lo = (a - hi.astype(F32)).astype(BF16)
    return hi, lo


def stack3(a):
    hi, lo = split(a)
    return jnp.concatenate([hi, lo, hi], axis=0)


def times_square(a, w):
    hi, lo = split(a)
    r = jnp.dot(jnp.concatenate([hi, lo], axis=1), w, preferred_element_type=F32)
    return r[:, :128] + r[:, 128:]


def dot(a, b):
    return jnp.dot(a, b, preferred_element_type=F32)


def row_at(y):
    return slice(y * STRIDE, y * STRIDE + N)


def z_forward(x_ref, t_ref, wz, steps):
    low = lane_iota() < N
    for p in steps:
        a = x_ref[:, p * 128 : p * 128 + 128]
        b = x_ref[:, (31 - p) * 128 : (32 - p) * 128]
        z = times_square(jnp.concatenate([jnp.where(low, a, b), jnp.where(low, b, a)], axis=0), wz)
        t_ref[row_at(2 * p), :] = z[:N]
        t_ref[row_at(2 * p + 1), :] = z[N:]


def x_either(a_ref, b_ref, lx):
    for p in range(16):
        a = jnp.concatenate([a_ref[row_at(2 * p), :], a_ref[row_at(2 * p + 1), :]], axis=1)
        r = dot(lx, stack3(a))
        b_ref[row_at(2 * p), :] = r[:, :128]
        b_ref[row_at(2 * p + 1), :] = r[:, 128:]


def z_back(t_ref, o_ref, wz, p):
    low = lane_iota() < N
    both = jnp.concatenate([t_ref[row_at(2 * p), :], t_ref[row_at(2 * p + 1), :]], axis=0)
    o = times_square(both, wz)
    a, b = o[:N], o[N:]
    o_ref[:, p * 128 : p * 128 + 128] = jnp.where(low, a, b)
    o_ref[:, (31 - p) * 128 : (32 - p) * 128] = jnp.where(low, b, a)


def pair_y(ly, a, b):
    low = lane_iota() < N
    r = dot(ly, stack3(jnp.concatenate([a, b], axis=1)))
    return (
        jnp.where(low, r[:32, :128], r[32:, :128]),
        jnp.where(low, r[:32, 128:], r[32:, 128:]),
    )


def orient_row(code):
    lane = lane_iota()
    rows = jnp.where(lane < N, 1.0, -1.0)
    cols = jnp.where(lane % 2 == 0, 1.0, -1.0)
    one = jnp.ones((1, 128), F32)
    return jnp.where(code % 2 == 1, rows, one) * jnp.where(code // 2 == 1, cols, one)


def face_sums(se, so, y, m, g_ref, add):
    low = lane_iota() < N
    swapped = pltpu.roll(y, N, 1)
    total, diff = y + swapped, y - swapped
    parts = [
        se - so,
        se + so,
        jnp.where(low, diff[:32], -diff[32:]),
        jnp.where(low, total[:32], total[32:]),
    ]
    for at, part in enumerate(parts):
        rows = slice(32 * at, 32 * at + 32)
        value = m * part
        g_ref[rows, :] = value + g_ref[rows, :] if add else value


def spread_traces(lam, m, lx_ref, ly_ref):
    low = lane_iota() < N
    scale = inject_scale * m
    xh, xl, yh, yl = (lam[32 * i : 32 * i + 32] for i in range(4))
    lx_ref[0] = scale * (xl + xh)
    lx_ref[1] = scale * (xl - xh)
    pe, po = scale * (yl + yh), scale * (yl - yh)
    ly_ref[0:32, :] = jnp.where(low, pe, pltpu.roll(po, N, 1))
    ly_ref[32:64, :] = jnp.where(low, pltpu.roll(pe, N, 1), po)


def trace_kernel(
    f_hbm, mod_h, codes, table_h, lx_h, ly_h, lyi_h, wz_h, mx_h, planes_h,
    x_out,
    mod, table, lx_c, ly_c, lyi_c, wz_c, mx_c, planes, u_out, g_out, tx_out, ty_out,
    xin, t_scr, x_scr, y_scr, face, lam, msend, mrecv, send, recv,
    in_sem, con_sem, msend_sem, mrecv_sem, send_sem, recv_sem,
):
    s, j = lax.axis_index("blk"), lax.axis_index("face")
    ns, nj = lax.axis_size("blk"), lax.axis_size("face")
    partner = [
        (lax.rem(s + ns - 1, ns), j),
        (lax.rem(s + 1, ns), j),
        (s, lax.rem(j + nj - 1, nj)),
        (s, lax.rem(j + 1, nj)),
    ]
    barrier = pltpu.get_barrier_semaphore()
    strips = [
        pltpu.make_async_copy(
            f_hbm.at[0, :, pl.ds(at * 1024, 1024)], xin.at[0, :, pl.ds(at * 1024, 1024)],
            in_sem.at[n],
        )
        for n, at in enumerate((0, 3, 1, 2))
    ]
    loads = [
        pltpu.make_async_copy(f_hbm.at[c], xin.at[c], in_sem.at[3 + c]) for c in range(1, COMPS)
    ]
    pairs = [
        (mod_h, mod), (table_h, table), (planes_h, planes),
        (wz_h, wz_c), (lx_h, lx_c), (ly_h, ly_c), (mx_h, mx_c), (lyi_h, lyi_c),
    ]
    small = [pltpu.make_async_copy(a, b, con_sem.at[i]) for i, (a, b) in enumerate(pairs)]
    for copy in small[:3]:
        copy.start()
    strips[0].start()
    strips[1].start()
    small[3].start()
    strips[2].start()
    strips[3].start()
    for copy in small[4:]:
        copy.start()
    for load in loads:
        load.start()
    recv[:, :, 0:2] = jnp.zeros((ITERS, COMPS, 2, 32, 128), F32)
    mrecv[0:2] = jnp.ones((2, 8, 128), F32)
    present = [s > 0, s < ns - 1, None, None]

    def where_present(d, action):
        if present[d] is None:
            action()
        else:
            pl.when(present[d])(action)

    def from_present(d, action):
        where_present(d ^ 1 if d < 2 else d, action)

    for d in range(4):
        where_present(
            d,
            lambda d=d: pl.semaphore_signal(
                barrier, inc=1, device_id=partner[d], device_id_type=MESH
            ),
        )

    for copy in small[:3]:
        copy.wait()
    row = lax.broadcasted_iota(jnp.int32, (8, 128), 0)
    moduli = [mod[0, 0, c] for c in range(COMPS)]
    msend[...] = jnp.where(row == 0, moduli[0], jnp.where(row == 1, moduli[1], moduli[2]))
    flip = orient_row(codes[0, 0])
    live_high = jnp.where(s < ns - 1, 1.0, 0.0).astype(F32)
    live_low = jnp.where(s > 0, 1.0, 0.0).astype(F32)
    omegas = step_weights()

    def fill(i, carry):
        ejk = planes[2]
        for c in range(COMPS):
            d = moduli[c] * (ejk + table[2, i]) + mass_shift
            r = pl.reciprocal(d, approx=True)
            g_out[c, i] = r * (2.0 - d * r)
        return carry

    lax.fori_loop(0, N, fill, 0, unroll=4)

    def mcopy(d):
        return pltpu.make_async_remote_copy(
            src_ref=msend, dst_ref=mrecv.at[d], send_sem=msend_sem.at[d],
            recv_sem=mrecv_sem.at[d], device_id=partner[d], device_id_type=MESH,
        )

    def gcopy(k, c, d):
        return pltpu.make_async_remote_copy(
            src_ref=send.at[k, c, d], dst_ref=recv.at[k, c, d], send_sem=send_sem.at[k, c, d],
            recv_sem=recv_sem.at[k, c, d], device_id=partner[d], device_id_type=MESH,
        )


    def send_faces(k, c):
        send[k, c, 0] = face[c, 32:64, :]
        send[k, c, 1] = face[c, 0:32, :] * flip
        send[k, c, 2] = face[c, 96:128, :]
        send[k, c, 3] = face[c, 64:96, :]
        for d in range(4):
            where_present(d, gcopy(k, c, d).start)

    def reduce_group(values, base, carry):
        se, so = carry
        cj = planes[0]
        sums = []
        for n, u in enumerate(values):
            weighted = table[0, base + n] * u
            if n % 2 == 0:
                se = se + weighted
            else:
                so = so + weighted
            w = cj * u
            sums.append((w[0:8] + w[8:16]) + (w[16:24] + w[24:32]))
        y = jnp.sum(jnp.stack(sums, axis=0), axis=1)
        y_scr[base : base + 8, :] = y
        return se, so

    zero = jnp.zeros((32, 128), F32)

    def forward(c):
        if c == 0:
            small[3].wait()
            strips[0].wait()
            strips[1].wait()
            z_forward(xin.at[c], t_scr, wz_c[...], range(8))
            strips[2].wait()
            strips[3].wait()
            z_forward(xin.at[c], t_scr, wz_c[...], range(8, 16))
            for copy in small[4:]:
                copy.wait()
        else:
            loads[c - 1].wait()
            z_forward(xin.at[c], t_scr, wz_c[...], range(16))
        x_either(t_scr, x_scr, lx_c[...])
        sums = (zero, zero)
        for base in range(0, N, 8):
            values = []
            for n in range(0, 8, 2):
                a = x_scr[pl.ds(base + n, 32, stride=STRIDE), :]
                b = x_scr[pl.ds(base + n + 1, 32, stride=STRIDE), :]
                for off, h in enumerate(pair_y(ly_c[...], a, b)):
                    u = h * g_out[c, base + n + off]
                    u_out[c, base + n + off] = u
                    values.append(u)
            sums = reduce_group(values, base, sums)
        face_sums(*sums, y_scr[...], moduli[c], face.at[c], False)
        if c == 0:
            pl.semaphore_wait(barrier, 4 - jnp.where(s > 0, 0, 1) - jnp.where(s < ns - 1, 0, 1))
            for d in range(4):
                where_present(d, mcopy(d).start)
        send_faces(0, c)

    def update(k, c):
        for d in range(4):
            from_present(d, gcopy(k, c, d).wait_recv)
        m = moduli[c]
        order = [0, 1, 2, 3]
        residues = []
        for at, d in enumerate(order):
            other = recv[k, c, d]
            if d == 0:
                other = other * flip
            inverse = 1.0 / (m + mrecv[d, c : c + 1, :])
            r = (face[c, 32 * at : 32 * at + 32, :] + other) * inverse
            if k > 0:
                r = r - lam[c, 32 * at : 32 * at + 32, :]
            if d == 0:
                r = r * live_high
            if d == 1:
                r = r * live_low
            residues.append(r)
        step = omegas[k] * times_square(jnp.concatenate(residues, axis=0), mx_c[...])
        new = step + lam[c] if k > 0 else step
        lam[c] = new
        spread_traces(new, m, tx_out.at[c], ty_out.at[c])

    def move(c):
        update(0, c)
        sums = (zero, zero)
        q0j = planes[1]
        for base in range(0, N, 8):
            values = []
            for i in range(base, base + 8):
                add = table[1, i] * tx_out[c, i % 2] + q0j * ty_out[c, i : i + 1, :]
                values.append(g_out[c, i] * add)
            sums = reduce_group(values, base, sums)
        face_sums(*sums, y_scr[...], moduli[c], face.at[c], True)
        send_faces(1, c)

    def back(c):
        update(1, c)
        q0j = planes[1]
        for i in range(0, N, 2):
            values = []
            for n in range(2):
                add = table[1, i + n] * tx_out[c, n] + q0j * ty_out[c, i + n : i + n + 1, :]
                values.append(u_out[c, i + n] + g_out[c, i + n] * add)
            a, b = pair_y(lyi_c[...], *values)
            t_scr[pl.ds(i, 32, stride=STRIDE), :] = a
            t_scr[pl.ds(i + 1, 32, stride=STRIDE), :] = b
        x_either(t_scr, x_out.at[c], lx_c[...])

    for c in range(COMPS):
        forward(c)
    for d in range(4):
        from_present(d, mcopy(d).wait_recv)
    for c in range(COMPS):
        move(c)
    for c in range(COMPS):
        back(c)
    for d in range(4):
        where_present(d, mcopy(d).wait_send)
    for k in range(ITERS):
        for c in range(COMPS):
            for d in range(4):
                where_present(d, gcopy(k, c, d).wait_send)


CHUNKS = 4


def back_kernel(x_ref, wz_c, out_hbm, o_scr, out_sem):
    def ocopy(c, chunk, side):
        first = chunk * 512 if side == 0 else 3584 - chunk * 512
        return pltpu.make_async_copy(
            o_scr.at[c, :, pl.ds(first, 512)],
            out_hbm.at[c, :, pl.ds(first, 512)],
            out_sem.at[c, chunk, side],
        )

    for c in range(COMPS):
        for chunk in range(CHUNKS):
            for p in range(4 * chunk, 4 * chunk + 4):
                z_back(x_ref.at[c], o_scr.at[c], wz_c[...], p)
            ocopy(c, chunk, 0).start()
            ocopy(c, chunk, 1).start()
    for c in range(COMPS):
        for chunk in range(CHUNKS):
            ocopy(c, chunk, 0).wait()
            ocopy(c, chunk, 1).wait()


def shards(forcing, modulus, orient_codes):
    lx, ly, lyi, wz, mx, table, planes = (jnp.asarray(a) for a in constants())
    f = forcing.reshape(COMPS, N, N * N)
    vmem = pl.BlockSpec(memory_space=pltpu.VMEM)
    smem = pl.BlockSpec(memory_space=pltpu.SMEM)
    hbm = pl.BlockSpec(memory_space=pltpu.HBM)
    spectral = (COMPS, N, N // 2, 128)
    x_back = pl.pallas_call(
        trace_kernel,
        out_shape=pltpu.VMEM((COMPS, 32 * STRIDE, 128), F32),
        in_specs=[hbm, hbm, smem] + [hbm] * 7,
        out_specs=vmem,
        scratch_shapes=[
            pltpu.SMEM((1, 1, COMPS), F32),
            pltpu.SMEM(table.shape, F32),
            pltpu.VMEM(lx.shape, BF16),
            pltpu.VMEM(ly.shape, BF16),
            pltpu.VMEM(lyi.shape, BF16),
            pltpu.VMEM(wz.shape, BF16),
            pltpu.VMEM(mx.shape, BF16),
            pltpu.VMEM(planes.shape, F32),
            pltpu.VMEM(spectral, F32),
            pltpu.VMEM(spectral, F32),
            pltpu.VMEM((COMPS, 2, 32, 128), F32),
            pltpu.VMEM((COMPS, N, 128), F32),
            pltpu.VMEM((COMPS, N, N * N), F32),
            pltpu.VMEM((32 * STRIDE, 128), F32),
            pltpu.VMEM((32 * STRIDE, 128), F32),
            pltpu.VMEM((N, 128), F32),
            pltpu.VMEM((COMPS, 128, 128), F32),
            pltpu.VMEM((COMPS, 128, 128), F32),
            pltpu.VMEM((8, 128), F32),
            pltpu.VMEM((4, 8, 128), F32),
            pltpu.VMEM((ITERS, COMPS, 4, 32, 128), F32),
            pltpu.VMEM((ITERS, COMPS, 4, 32, 128), F32),
            pltpu.SemaphoreType.DMA((6,)),
            pltpu.SemaphoreType.DMA((8,)),
            pltpu.SemaphoreType.DMA((4,)),
            pltpu.SemaphoreType.DMA((4,)),
            pltpu.SemaphoreType.DMA((ITERS, COMPS, 4)),
            pltpu.SemaphoreType.DMA((ITERS, COMPS, 4)),
        ],
        compiler_params=pltpu.CompilerParams(
            collective_id=0, has_side_effects=True, vmem_limit_bytes=40 * 2**20
        ),
        cost_estimate=pl.CostEstimate(flops=2 * 10**9, bytes_accessed=3 * 2**20, transcendentals=0),
        name="traces",
    )(in_hbm(f), in_hbm(modulus), orient_codes, *(in_hbm(a) for a in (table, lx, ly, lyi, wz, mx, planes)))
    out = pl.pallas_call(
        back_kernel,
        out_shape=jax.ShapeDtypeStruct((COMPS, N, N * N), F32),
        in_specs=[vmem] * 2,
        out_specs=hbm,
        scratch_shapes=[
            pltpu.VMEM((COMPS, N, N * N), F32),
            pltpu.SemaphoreType.DMA((COMPS, CHUNKS, 2)),
        ],
        compiler_params=pltpu.CompilerParams(vmem_limit_bytes=40 * 2**20),
        cost_estimate=pl.CostEstimate(flops=2 * 10**9, bytes_accessed=3 * 2**20, transcendentals=0),
        name="back",
    )(x_back, wz)
    return out.reshape(forcing.shape)


def solution(mesh):
    placed = (P("blk", "face", None, None, None), P("blk", "face", None), P("blk", "face"))
    return jax.shard_map(
        shards,
        mesh=mesh,
        in_specs=placed,
        out_specs=P("blk", "face", None, None, None),
        check_vma=False,
    )
```

```python
import functools
import math

import jax
import jax.numpy as jnp
import ml_dtypes
import numpy as np
from jax import lax
from jax.experimental import pallas as pl
from jax.experimental.pallas import tpu as pltpu
from jax.sharding import PartitionSpec as P

N = 64
ITERS = 2
COMPS = 3
STRIDE = 72
MESH = pl.DeviceIdType.MESH
F32 = jnp.float32
BF16 = jnp.bfloat16
mass_shift = 0.02
inject_scale = 2.0
traction_mix = 0.5
penalty_mix = 0.25
lower_edge = 0.3
upper_edge = 1.5


def in_hbm(a):
    return pltpu.with_memory_space_constraint(a, pltpu.HBM)


def split_np(a):
    a = np.asarray(a, np.float32)
    hi = a.astype(ml_dtypes.bfloat16)
    lo = (a - hi.astype(np.float32)).astype(ml_dtypes.bfloat16)
    return hi, lo


def rows3(a):
    hi, lo = split_np(a)
    return np.concatenate([hi, hi, lo], axis=1)


def square3(a):
    hi, lo = split_np(a)
    top = np.concatenate([hi, lo], axis=1)
    bottom = np.concatenate([hi, np.zeros_like(hi)], axis=1)
    return np.concatenate([top, bottom], axis=0)


def constants():
    n = np.arange(1, N + 1, dtype=np.float64)
    q = math.sqrt(2.0 / (N + 1)) * np.sin(math.pi * n[:, None] * n[None, :] / (N + 1))
    e = 2.0 - 2.0 * np.cos(math.pi * n / (N + 1))
    tangent = np.diag(np.full(N, -2.0)) + np.diag(np.ones(N - 1), 1) + np.diag(np.ones(N - 1), -1)
    tangent[0, 0] = tangent[-1, -1] = -1.0
    smooth = np.eye(N) + penalty_mix * (q @ tangent @ q)
    half = N // 2
    sign = (-1.0) ** np.arange(half)
    fold = np.block([[q, q], [q, -q]])
    even, odd = q[0::2, :half], q[1::2, :half] * sign[None, :]
    lx = rows3(q)
    ly = rows3(np.concatenate([even, odd], axis=0))
    lyi = rows3(np.concatenate([even.T, odd.T], axis=0))
    wz = square3(fold)
    mx = square3(np.kron(np.eye(2), smooth))
    normal = q[0] + traction_mix * (11.0 / 6.0 * q[0] - 3.0 * q[1] + 1.5 * q[2] - q[3] / 3.0)
    table = np.stack([normal, q[0], e]).astype(np.float32)
    spread = lambda v: np.repeat(v.reshape(half, 2), N, axis=1)
    planes = np.stack(
        [spread(normal), spread(q[0]), spread(e) + np.tile(e, 2)[None, :]]
    ).astype(np.float32)
    return lx, ly, lyi, wz, mx, table, planes


def step_weights():
    mid = 0.5 * (upper_edge + lower_edge)
    radius = 0.5 * (upper_edge - lower_edge)
    return [
        1.0 / (mid + radius * math.cos(math.pi * (2 * k + 1) / (2 * ITERS))) for k in range(ITERS)
    ]


def lane_iota():
    return lax.broadcasted_iota(jnp.int32, (1, 128), 1)


def split(a):
    hi = a.astype(BF16)
    lo = (a - hi.astype(F32)).astype(BF16)
    return hi, lo


def stack3(a):
    hi, lo = split(a)
    return jnp.concatenate([hi, lo, hi], axis=0)


def times_square(a, w):
    hi, lo = split(a)
    r = jnp.dot(jnp.concatenate([hi, lo], axis=1), w, preferred_element_type=F32)
    return r[:, :128] + r[:, 128:]


def dot(a, b):
    return jnp.dot(a, b, preferred_element_type=F32)


def row_at(y):
    return slice(y * STRIDE, y * STRIDE + N)


def z_forward(x_ref, t_ref, wz, steps):
    low = lane_iota() < N
    for p in steps:
        a = x_ref[:, p * 128 : p * 128 + 128]
        b = x_ref[:, (31 - p) * 128 : (32 - p) * 128]
        z = times_square(jnp.concatenate([jnp.where(low, a, b), jnp.where(low, b, a)], axis=0), wz)
        t_ref[row_at(2 * p), :] = z[:N]
        t_ref[row_at(2 * p + 1), :] = z[N:]


def x_either(a_ref, b_ref, lx):
    for p in range(16):
        a = jnp.concatenate([a_ref[row_at(2 * p), :], a_ref[row_at(2 * p + 1), :]], axis=1)
        r = dot(lx, stack3(a))
        b_ref[row_at(2 * p), :] = r[:, :128]
        b_ref[row_at(2 * p + 1), :] = r[:, 128:]


def z_back(t_ref, o_ref, wz, p):
    low = lane_iota() < N
    both = jnp.concatenate([t_ref[row_at(2 * p), :], t_ref[row_at(2 * p + 1), :]], axis=0)
    o = times_square(both, wz)
    a, b = o[:N], o[N:]
    o_ref[:, p * 128 : p * 128 + 128] = jnp.where(low, a, b)
    o_ref[:, (31 - p) * 128 : (32 - p) * 128] = jnp.where(low, b, a)


def pair_y(ly, a, b):
    low = lane_iota() < N
    r = dot(ly, stack3(jnp.concatenate([a, b], axis=1)))
    return (
        jnp.where(low, r[:32, :128], r[32:, :128]),
        jnp.where(low, r[:32, 128:], r[32:, 128:]),
    )


def orient_row(code):
    lane = lane_iota()
    rows = jnp.where(lane < N, 1.0, -1.0)
    cols = jnp.where(lane % 2 == 0, 1.0, -1.0)
    one = jnp.ones((1, 128), F32)
    return jnp.where(code % 2 == 1, rows, one) * jnp.where(code // 2 == 1, cols, one)


def face_sums(se, so, y, m, g_ref, add):
    low = lane_iota() < N
    swapped = pltpu.roll(y, N, 1)
    total, diff = y + swapped, y - swapped
    parts = [
        se - so,
        se + so,
        jnp.where(low, diff[:32], -diff[32:]),
        jnp.where(low, total[:32], total[32:]),
    ]
    for at, part in enumerate(parts):
        rows = slice(32 * at, 32 * at + 32)
        value = m * part
        g_ref[rows, :] = value + g_ref[rows, :] if add else value


def spread_traces(lam, m, lx_ref, ly_ref):
    low = lane_iota() < N
    scale = inject_scale * m
    xh, xl, yh, yl = (lam[32 * i : 32 * i + 32] for i in range(4))
    lx_ref[0] = scale * (xl + xh)
    lx_ref[1] = scale * (xl - xh)
    pe, po = scale * (yl + yh), scale * (yl - yh)
    ly_ref[0:32, :] = jnp.where(low, pe, pltpu.roll(po, N, 1))
    ly_ref[32:64, :] = jnp.where(low, pltpu.roll(pe, N, 1), po)


def trace_kernel(
    f_hbm, mod_h, codes, table_h, lx_h, ly_h, lyi_h, wz_h, mx_h, planes_h,
    y_out,
    mod, table, lx_c, ly_c, lyi_c, wz_c, mx_c, planes, u_out, g_out, tx_out, ty_out,
    xin, t_scr, x_scr, y_scr, face, lam, msend, mrecv, send, recv,
    in_sem, con_sem, msend_sem, mrecv_sem, send_sem, recv_sem,
):
    s, j = lax.axis_index("blk"), lax.axis_index("face")
    ns, nj = lax.axis_size("blk"), lax.axis_size("face")
    partner = [
        (lax.rem(s + ns - 1, ns), j),
        (lax.rem(s + 1, ns), j),
        (s, lax.rem(j + nj - 1, nj)),
        (s, lax.rem(j + 1, nj)),
    ]
    barrier = pltpu.get_barrier_semaphore()
    strips = [
        pltpu.make_async_copy(
            f_hbm.at[0, :, pl.ds(at * 1024, 1024)], xin.at[0, :, pl.ds(at * 1024, 1024)],
            in_sem.at[n],
        )
        for n, at in enumerate((0, 3, 1, 2))
    ]
    loads = [
        pltpu.make_async_copy(f_hbm.at[c], xin.at[c], in_sem.at[3 + c]) for c in range(1, COMPS)
    ]
    pairs = [
        (mod_h, mod), (table_h, table), (planes_h, planes),
        (wz_h, wz_c), (lx_h, lx_c), (ly_h, ly_c), (mx_h, mx_c), (lyi_h, lyi_c),
    ]
    small = [pltpu.make_async_copy(a, b, con_sem.at[i]) for i, (a, b) in enumerate(pairs)]
    strips[0].start()
    strips[1].start()
    for copy in small[:4]:
        copy.start()
    strips[2].start()
    strips[3].start()
    for copy in small[4:]:
        copy.start()
    for load in loads:
        load.start()
    recv[:, :, 0:2] = jnp.zeros((ITERS, COMPS, 2, 32, 128), F32)
    mrecv[0:2] = jnp.ones((2, 8, 128), F32)
    present = [s > 0, s < ns - 1, None, None]

    def where_present(d, action):
        if present[d] is None:
            action()
        else:
            pl.when(present[d])(action)

    def from_present(d, action):
        where_present(d ^ 1 if d < 2 else d, action)

    for d in range(4):
        where_present(
            d,
            lambda d=d: pl.semaphore_signal(
                barrier, inc=1, device_id=partner[d], device_id_type=MESH
            ),
        )

    for copy in small[:3]:
        copy.wait()
    row = lax.broadcasted_iota(jnp.int32, (8, 128), 0)
    moduli = [mod[0, 0, c] for c in range(COMPS)]
    msend[...] = jnp.where(row == 0, moduli[0], jnp.where(row == 1, moduli[1], moduli[2]))
    flip = orient_row(codes[0, 0])
    live_high = jnp.where(s < ns - 1, 1.0, 0.0).astype(F32)
    live_low = jnp.where(s > 0, 1.0, 0.0).astype(F32)
    omegas = step_weights()

    def gain(c, i):
        d = (moduli[c] * planes[2] + mass_shift) + moduli[c] * table[2, i]
        r = pl.reciprocal(d, approx=True)
        return r * (2.0 - d * r)

    def fill(i, carry):
        g_out[0, i] = gain(0, i)
        return carry

    lax.fori_loop(0, N, fill, 0, unroll=8)

    def mcopy(d):
        return pltpu.make_async_remote_copy(
            src_ref=msend, dst_ref=mrecv.at[d], send_sem=msend_sem.at[d],
            recv_sem=mrecv_sem.at[d], device_id=partner[d], device_id_type=MESH,
        )

    def gcopy(k, c, d):
        return pltpu.make_async_remote_copy(
            src_ref=send.at[k, c, d], dst_ref=recv.at[k, c, d], send_sem=send_sem.at[k, c, d],
            recv_sem=recv_sem.at[k, c, d], device_id=partner[d], device_id_type=MESH,
        )


    def send_faces(k, c):
        send[k, c, 0] = face[c, 32:64, :]
        send[k, c, 1] = face[c, 0:32, :] * flip
        send[k, c, 2] = face[c, 96:128, :]
        send[k, c, 3] = face[c, 64:96, :]
        for d in range(4):
            where_present(d, gcopy(k, c, d).start)

    def reduce_group(values, base, carry):
        se, so = carry
        cj = planes[0]
        sums = []
        for n, u in enumerate(values):
            weighted = table[0, base + n] * u
            if n % 2 == 0:
                se = se + weighted
            else:
                so = so + weighted
            w = cj * u
            sums.append((w[0:8] + w[8:16]) + (w[16:24] + w[24:32]))
        y = jnp.sum(jnp.stack(sums, axis=0), axis=1)
        y_scr[base : base + 8, :] = y
        return se, so

    zero = jnp.zeros((32, 128), F32)

    def forward(c):
        if c == 0:
            small[3].wait()
            strips[0].wait()
            strips[1].wait()
            z_forward(xin.at[c], t_scr, wz_c[...], range(8))
            strips[2].wait()
            strips[3].wait()
            z_forward(xin.at[c], t_scr, wz_c[...], range(8, 16))
            for copy in small[4:]:
                copy.wait()
        else:
            loads[c - 1].wait()
            z_forward(xin.at[c], t_scr, wz_c[...], range(16))
        x_either(t_scr, x_scr, lx_c[...])
        sums = (zero, zero)
        for base in range(0, N, 8):
            values = []
            for n in range(0, 8, 2):
                a = x_scr[pl.ds(base + n, 32, stride=STRIDE), :]
                b = x_scr[pl.ds(base + n + 1, 32, stride=STRIDE), :]
                for off, h in enumerate(pair_y(ly_c[...], a, b)):
                    i = base + n + off
                    if c > 0:
                        g_out[c, i] = gain(c, i)
                    u = h * g_out[c, i]
                    u_out[c, i] = u
                    values.append(u)
            sums = reduce_group(values, base, sums)
        face_sums(*sums, y_scr[...], moduli[c], face.at[c], False)
        if c == 0:
            pl.semaphore_wait(barrier, 4 - jnp.where(s > 0, 0, 1) - jnp.where(s < ns - 1, 0, 1))
            for d in range(4):
                where_present(d, mcopy(d).start)
        send_faces(0, c)

    def arrived(k, c):
        for d in range(4):
            from_present(d, gcopy(k, c, d).wait_recv)

    def update(k, c):
        m = moduli[c]
        order = [0, 1, 2, 3]
        residues = []
        for at, d in enumerate(order):
            other = recv[k, c, d]
            if d == 0:
                other = other * flip
            inverse = 1.0 / (m + mrecv[d, c : c + 1, :])
            r = (face[c, 32 * at : 32 * at + 32, :] + other) * inverse
            if k > 0:
                r = r - lam[c, 32 * at : 32 * at + 32, :]
            if d == 0:
                r = r * live_high
            if d == 1:
                r = r * live_low
            residues.append(r)
        step = omegas[k] * times_square(jnp.concatenate(residues, axis=0), mx_c[...])
        new = step + lam[c] if k > 0 else step
        lam[c] = new
        spread_traces(new, m, tx_out.at[c], ty_out.at[c])

    def move(c):
        arrived(0, c)
        update(0, c)
        sums = (zero, zero)
        q0j = planes[1]
        for base in range(0, N, 8):
            values = []
            for i in range(base, base + 8):
                add = table[1, i] * tx_out[c, i % 2] + q0j * ty_out[c, i : i + 1, :]
                values.append(g_out[c, i] * add)
            sums = reduce_group(values, base, sums)
        face_sums(*sums, y_scr[...], moduli[c], face.at[c], True)
        send_faces(1, c)

    def back(c):
        q0j = planes[1]
        for i in range(0, N, 2):
            values = []
            for n in range(2):
                add = table[1, i + n] * tx_out[c, n] + q0j * ty_out[c, i + n : i + n + 1, :]
                values.append(u_out[c, i + n] + g_out[c, i + n] * add)
            a, b = pair_y(lyi_c[...], *values)
            y_out[c, pl.ds(i, 32, stride=STRIDE), :] = a
            y_out[c, pl.ds(i + 1, 32, stride=STRIDE), :] = b

    for c in range(COMPS):
        forward(c)
    for d in range(4):
        from_present(d, mcopy(d).wait_recv)
    for c in range(COMPS):
        move(c)
    arrived(1, 0)
    update(1, 0)
    for c in range(COMPS):
        if c + 1 < COMPS:
            arrived(1, c + 1)
            update(1, c + 1)
        back(c)
    for d in range(4):
        where_present(d, mcopy(d).wait_send)
    for k in range(ITERS):
        for c in range(COMPS):
            for d in range(4):
                where_present(d, gcopy(k, c, d).wait_send)


CHUNKS = 4


def back_kernel(y_ref, lx_c, wz_c, out_hbm, x_scr, o_scr, out_sem):
    def ocopy(c, chunk, side):
        first = chunk * 512 if side == 0 else 3584 - chunk * 512
        return pltpu.make_async_copy(
            o_scr.at[c, :, pl.ds(first, 512)],
            out_hbm.at[c, :, pl.ds(first, 512)],
            out_sem.at[c, chunk, side],
        )

    for c in range(COMPS):
        x_either(y_ref.at[c], x_scr.at[c], lx_c[...])
        for chunk in range(CHUNKS):
            for p in range(4 * chunk, 4 * chunk + 4):
                z_back(x_scr.at[c], o_scr.at[c], wz_c[...], p)
            ocopy(c, chunk, 0).start()
            ocopy(c, chunk, 1).start()
    for c in range(COMPS):
        for chunk in range(CHUNKS):
            ocopy(c, chunk, 0).wait()
            ocopy(c, chunk, 1).wait()


def shards(forcing, modulus, orient_codes):
    lx, ly, lyi, wz, mx, table, planes = (jnp.asarray(a) for a in constants())
    f = forcing.reshape(COMPS, N, N * N)
    vmem = pl.BlockSpec(memory_space=pltpu.VMEM)
    smem = pl.BlockSpec(memory_space=pltpu.SMEM)
    hbm = pl.BlockSpec(memory_space=pltpu.HBM)
    spectral = (COMPS, N, N // 2, 128)
    y_back = pl.pallas_call(
        trace_kernel,
        out_shape=pltpu.VMEM((COMPS, 32 * STRIDE, 128), F32),
        in_specs=[hbm, hbm, smem] + [hbm] * 7,
        out_specs=vmem,
        scratch_shapes=[
            pltpu.SMEM((1, 1, COMPS), F32),
            pltpu.SMEM(table.shape, F32),
            pltpu.VMEM(lx.shape, BF16),
            pltpu.VMEM(ly.shape, BF16),
            pltpu.VMEM(lyi.shape, BF16),
            pltpu.VMEM(wz.shape, BF16),
            pltpu.VMEM(mx.shape, BF16),
            pltpu.VMEM(planes.shape, F32),
            pltpu.VMEM(spectral, F32),
            pltpu.VMEM(spectral, F32),
            pltpu.VMEM((COMPS, 2, 32, 128), F32),
            pltpu.VMEM((COMPS, N, 128), F32),
            pltpu.VMEM((COMPS, N, N * N), F32),
            pltpu.VMEM((32 * STRIDE, 128), F32),
            pltpu.VMEM((32 * STRIDE, 128), F32),
            pltpu.VMEM((N, 128), F32),
            pltpu.VMEM((COMPS, 128, 128), F32),
            pltpu.VMEM((COMPS, 128, 128), F32),
            pltpu.VMEM((8, 128), F32),
            pltpu.VMEM((4, 8, 128), F32),
            pltpu.VMEM((ITERS, COMPS, 4, 32, 128), F32),
            pltpu.VMEM((ITERS, COMPS, 4, 32, 128), F32),
            pltpu.SemaphoreType.DMA((6,)),
            pltpu.SemaphoreType.DMA((8,)),
            pltpu.SemaphoreType.DMA((4,)),
            pltpu.SemaphoreType.DMA((4,)),
            pltpu.SemaphoreType.DMA((ITERS, COMPS, 4)),
            pltpu.SemaphoreType.DMA((ITERS, COMPS, 4)),
        ],
        compiler_params=pltpu.CompilerParams(
            collective_id=0, has_side_effects=True, vmem_limit_bytes=40 * 2**20
        ),
        cost_estimate=pl.CostEstimate(flops=2 * 10**9, bytes_accessed=3 * 2**20, transcendentals=0),
        name="traces",
    )(in_hbm(f), in_hbm(modulus), orient_codes, *(in_hbm(a) for a in (table, lx, ly, lyi, wz, mx, planes)))
    out = pl.pallas_call(
        back_kernel,
        out_shape=jax.ShapeDtypeStruct((COMPS, N, N * N), F32),
        in_specs=[vmem] * 3,
        out_specs=hbm,
        scratch_shapes=[
            pltpu.VMEM((COMPS, 32 * STRIDE, 128), F32),
            pltpu.VMEM((COMPS, N, N * N), F32),
            pltpu.SemaphoreType.DMA((COMPS, CHUNKS, 2)),
        ],
        compiler_params=pltpu.CompilerParams(vmem_limit_bytes=40 * 2**20),
        cost_estimate=pl.CostEstimate(flops=2 * 10**9, bytes_accessed=3 * 2**20, transcendentals=0),
        name="back",
    )(y_back, lx, wz)
    return out.reshape(forcing.shape)


def solution(mesh):
    placed = (P("blk", "face", None, None, None), P("blk", "face", None), P("blk", "face"))
    return jax.shard_map(
        shards,
        mesh=mesh,
        in_specs=placed,
        out_specs=P("blk", "face", None, None, None),
        check_vma=False,
    )
```

```python
import functools
import math

import jax
import jax.numpy as jnp
import ml_dtypes
import numpy as np
from jax import lax
from jax.experimental import pallas as pl
from jax.experimental.pallas import tpu as pltpu
from jax.sharding import PartitionSpec as P

N = 64
ITERS = 2
COMPS = 3
STRIDE = 72
MESH = pl.DeviceIdType.MESH
F32 = jnp.float32
BF16 = jnp.bfloat16
mass_shift = 0.02
inject_scale = 2.0
traction_mix = 0.5
penalty_mix = 0.25
lower_edge = 0.3
upper_edge = 1.5


def in_hbm(a):
    return pltpu.with_memory_space_constraint(a, pltpu.HBM)


def split_np(a):
    a = np.asarray(a, np.float32)
    hi = a.astype(ml_dtypes.bfloat16)
    lo = (a - hi.astype(np.float32)).astype(ml_dtypes.bfloat16)
    return hi, lo


def rows3(a):
    hi, lo = split_np(a)
    return np.concatenate([hi, hi, lo], axis=1)


def square3(a):
    hi, lo = split_np(a)
    top = np.concatenate([hi, lo], axis=1)
    bottom = np.concatenate([hi, np.zeros_like(hi)], axis=1)
    return np.concatenate([top, bottom], axis=0)


def constants():
    n = np.arange(1, N + 1, dtype=np.float64)
    q = math.sqrt(2.0 / (N + 1)) * np.sin(math.pi * n[:, None] * n[None, :] / (N + 1))
    e = 2.0 - 2.0 * np.cos(math.pi * n / (N + 1))
    tangent = np.diag(np.full(N, -2.0)) + np.diag(np.ones(N - 1), 1) + np.diag(np.ones(N - 1), -1)
    tangent[0, 0] = tangent[-1, -1] = -1.0
    smooth = np.eye(N) + penalty_mix * (q @ tangent @ q)
    half = N // 2
    sign = (-1.0) ** np.arange(half)
    fold = np.block([[q, q], [q, -q]])
    even, odd = q[0::2, :half], q[1::2, :half] * sign[None, :]
    lx = rows3(q)
    ly = rows3(np.concatenate([even, odd], axis=0))
    lyi = rows3(np.concatenate([even.T, odd.T], axis=0))
    wz = square3(fold)
    mx = square3(np.kron(np.eye(2), smooth))
    normal = q[0] + traction_mix * (11.0 / 6.0 * q[0] - 3.0 * q[1] + 1.5 * q[2] - q[3] / 3.0)
    table = np.stack([normal, q[0], e]).astype(np.float32)
    spread = lambda v: np.repeat(v.reshape(half, 2), N, axis=1)
    planes = np.stack(
        [spread(normal), spread(q[0]), spread(e) + np.tile(e, 2)[None, :]]
    ).astype(np.float32)
    return lx, ly, lyi, wz, mx, table, planes


def step_weights():
    mid = 0.5 * (upper_edge + lower_edge)
    radius = 0.5 * (upper_edge - lower_edge)
    return [
        1.0 / (mid + radius * math.cos(math.pi * (2 * k + 1) / (2 * ITERS))) for k in range(ITERS)
    ]


def lane_iota():
    return lax.broadcasted_iota(jnp.int32, (1, 128), 1)


def split(a):
    hi = a.astype(BF16)
    lo = (a - hi.astype(F32)).astype(BF16)
    return hi, lo


def stack3(a):
    hi, lo = split(a)
    return jnp.concatenate([hi, lo, hi], axis=0)


def times_square(a, w):
    hi, lo = split(a)
    r = jnp.dot(jnp.concatenate([hi, lo], axis=1), w, preferred_element_type=F32)
    return r[:, :128] + r[:, 128:]


def dot(a, b):
    return jnp.dot(a, b, preferred_element_type=F32)


def row_at(y):
    return slice(y * STRIDE, y * STRIDE + N)


def z_forward(x_ref, t_ref, wz, steps):
    low = lane_iota() < N
    for p in steps:
        a = x_ref[:, p * 128 : p * 128 + 128]
        b = x_ref[:, (31 - p) * 128 : (32 - p) * 128]
        z = times_square(jnp.concatenate([jnp.where(low, a, b), jnp.where(low, b, a)], axis=0), wz)
        t_ref[row_at(2 * p), :] = z[:N]
        t_ref[row_at(2 * p + 1), :] = z[N:]


def x_either(a_ref, b_ref, lx):
    for p in range(16):
        a = jnp.concatenate([a_ref[row_at(2 * p), :], a_ref[row_at(2 * p + 1), :]], axis=1)
        r = dot(lx, stack3(a))
        b_ref[row_at(2 * p), :] = r[:, :128]
        b_ref[row_at(2 * p + 1), :] = r[:, 128:]


def z_back(t_ref, o_ref, wz, p):
    low = lane_iota() < N
    both = jnp.concatenate([t_ref[row_at(2 * p), :], t_ref[row_at(2 * p + 1), :]], axis=0)
    o = times_square(both, wz)
    a, b = o[:N], o[N:]
    o_ref[:, p * 128 : p * 128 + 128] = jnp.where(low, a, b)
    o_ref[:, (31 - p) * 128 : (32 - p) * 128] = jnp.where(low, b, a)


def pair_y(ly, a, b):
    low = lane_iota() < N
    r = dot(ly, stack3(jnp.concatenate([a, b], axis=1)))
    return (
        jnp.where(low, r[:32, :128], r[32:, :128]),
        jnp.where(low, r[:32, 128:], r[32:, 128:]),
    )


def orient_row(code):
    lane = lane_iota()
    rows = jnp.where(lane < N, 1.0, -1.0)
    cols = jnp.where(lane % 2 == 0, 1.0, -1.0)
    one = jnp.ones((1, 128), F32)
    return jnp.where(code % 2 == 1, rows, one) * jnp.where(code // 2 == 1, cols, one)


def face_sums(se, so, y, m, g_ref, add):
    low = lane_iota() < N
    swapped = pltpu.roll(y, N, 1)
    total, diff = y + swapped, y - swapped
    parts = [
        se - so,
        se + so,
        jnp.where(low, diff[:32], -diff[32:]),
        jnp.where(low, total[:32], total[32:]),
    ]
    for at, part in enumerate(parts):
        rows = slice(32 * at, 32 * at + 32)
        value = m * part
        g_ref[rows, :] = value + g_ref[rows, :] if add else value


def spread_traces(lam, m, lx_ref, ly_ref):
    low = lane_iota() < N
    scale = inject_scale * m
    xh, xl, yh, yl = (lam[32 * i : 32 * i + 32] for i in range(4))
    lx_ref[0] = scale * (xl + xh)
    lx_ref[1] = scale * (xl - xh)
    pe, po = scale * (yl + yh), scale * (yl - yh)
    ly_ref[0:32, :] = jnp.where(low, pe, pltpu.roll(po, N, 1))
    ly_ref[32:64, :] = jnp.where(low, pltpu.roll(pe, N, 1), po)


def trace_kernel(
    f_hbm, mod_h, codes, table_h, lx_h, ly_h, lyi_h, wz_h, mx_h, planes_h,
    x_out, o_out,
    mod, table, lx_c, ly_c, lyi_c, wz_c, mx_c, planes, u_out, g_out, tx_out, ty_out,
    xin, t_scr, x_scr, y_scr, face, lam, msend, mrecv, send, recv,
    in_sem, con_sem, msend_sem, mrecv_sem, send_sem, recv_sem,
):
    s, j = lax.axis_index("blk"), lax.axis_index("face")
    ns, nj = lax.axis_size("blk"), lax.axis_size("face")
    partner = [
        (lax.rem(s + ns - 1, ns), j),
        (lax.rem(s + 1, ns), j),
        (s, lax.rem(j + nj - 1, nj)),
        (s, lax.rem(j + 1, nj)),
    ]
    barrier = pltpu.get_barrier_semaphore()
    strips = [
        pltpu.make_async_copy(
            f_hbm.at[0, :, pl.ds(at * 1024, 1024)], xin.at[0, :, pl.ds(at * 1024, 1024)],
            in_sem.at[n],
        )
        for n, at in enumerate((0, 3, 1, 2))
    ]
    loads = [
        pltpu.make_async_copy(f_hbm.at[c], xin.at[c], in_sem.at[3 + c]) for c in range(1, COMPS)
    ]
    pairs = [
        (mod_h, mod), (table_h, table), (planes_h, planes),
        (wz_h, wz_c), (lx_h, lx_c), (ly_h, ly_c), (mx_h, mx_c), (lyi_h, lyi_c),
    ]
    small = [pltpu.make_async_copy(a, b, con_sem.at[i]) for i, (a, b) in enumerate(pairs)]
    strips[0].start()
    strips[1].start()
    for copy in small[:4]:
        copy.start()
    strips[2].start()
    strips[3].start()
    for copy in small[4:]:
        copy.start()
    for load in loads:
        load.start()
    recv[:, :, 0:2] = jnp.zeros((ITERS, COMPS, 2, 32, 128), F32)
    mrecv[0:2] = jnp.ones((2, 8, 128), F32)
    present = [s > 0, s < ns - 1, None, None]

    def where_present(d, action):
        if present[d] is None:
            action()
        else:
            pl.when(present[d])(action)

    def from_present(d, action):
        where_present(d ^ 1 if d < 2 else d, action)

    for d in range(4):
        where_present(
            d,
            lambda d=d: pl.semaphore_signal(
                barrier, inc=1, device_id=partner[d], device_id_type=MESH
            ),
        )

    for copy in small[:3]:
        copy.wait()
    row = lax.broadcasted_iota(jnp.int32, (8, 128), 0)
    moduli = [mod[0, 0, c] for c in range(COMPS)]
    msend[...] = jnp.where(row == 0, moduli[0], jnp.where(row == 1, moduli[1], moduli[2]))
    flip = orient_row(codes[0, 0])
    live_high = jnp.where(s < ns - 1, 1.0, 0.0).astype(F32)
    live_low = jnp.where(s > 0, 1.0, 0.0).astype(F32)
    omegas = step_weights()

    def gain(c, i):
        d = (moduli[c] * planes[2] + mass_shift) + moduli[c] * table[2, i]
        r = pl.reciprocal(d, approx=True)
        return r * (2.0 - d * r)

    def fill(i, carry):
        g_out[0, i] = gain(0, i)
        return carry

    lax.fori_loop(0, N, fill, 0, unroll=8)

    def mcopy(d):
        return pltpu.make_async_remote_copy(
            src_ref=msend, dst_ref=mrecv.at[d], send_sem=msend_sem.at[d],
            recv_sem=mrecv_sem.at[d], device_id=partner[d], device_id_type=MESH,
        )

    def gcopy(k, c, d):
        return pltpu.make_async_remote_copy(
            src_ref=send.at[k, c, d], dst_ref=recv.at[k, c, d], send_sem=send_sem.at[k, c, d],
            recv_sem=recv_sem.at[k, c, d], device_id=partner[d], device_id_type=MESH,
        )


    def send_faces(k, c):
        send[k, c, 0] = face[c, 32:64, :]
        send[k, c, 1] = face[c, 0:32, :] * flip
        send[k, c, 2] = face[c, 96:128, :]
        send[k, c, 3] = face[c, 64:96, :]
        for d in range(4):
            where_present(d, gcopy(k, c, d).start)

    def reduce_one(u, i, sums, rows):
        weighted = table[0, i] * u
        sums[i % 2] = weighted if sums[i % 2] is None else sums[i % 2] + weighted
        w = planes[0] * u
        rows.append((w[0:8] + w[8:16]) + (w[16:24] + w[24:32]))
        if len(rows) == 8:
            y_scr[i - 7 : i + 1, :] = jnp.sum(jnp.stack(rows, axis=0), axis=1)
            rows.clear()

    def forward(c):
        if c == 0:
            small[3].wait()
            strips[0].wait()
            strips[1].wait()
            z_forward(xin.at[c], t_scr, wz_c[...], range(8))
            strips[2].wait()
            strips[3].wait()
            z_forward(xin.at[c], t_scr, wz_c[...], range(8, 16))
            for copy in small[4:]:
                copy.wait()
        else:
            loads[c - 1].wait()
            z_forward(xin.at[c], t_scr, wz_c[...], range(16))
        x_either(t_scr, x_scr, lx_c[...])
        sums, rows = [None, None], []
        for first in range(0, N, 2):
            a = x_scr[pl.ds(first, 32, stride=STRIDE), :]
            b = x_scr[pl.ds(first + 1, 32, stride=STRIDE), :]
            for i, h in zip((first, first + 1), pair_y(ly_c[...], a, b)):
                g = g_out[0, i] if c == 0 else gain(c, i)
                if c > 0:
                    g_out[c, i] = g
                u = h * g
                u_out[c, i] = u
                reduce_one(u, i, sums, rows)
        face_sums(*sums, y_scr[...], moduli[c], face.at[c], False)
        if c == 0:
            pl.semaphore_wait(barrier, 4 - jnp.where(s > 0, 0, 1) - jnp.where(s < ns - 1, 0, 1))
            for d in range(4):
                where_present(d, mcopy(d).start)
        send_faces(0, c)

    def arrived(k, c):
        for d in range(4):
            from_present(d, gcopy(k, c, d).wait_recv)

    def update(k, c):
        m = moduli[c]
        order = [0, 1, 2, 3]
        residues = []
        for at, d in enumerate(order):
            other = recv[k, c, d]
            if d == 0:
                other = other * flip
            inverse = 1.0 / (m + mrecv[d, c : c + 1, :])
            r = (face[c, 32 * at : 32 * at + 32, :] + other) * inverse
            if k > 0:
                r = r - lam[c, 32 * at : 32 * at + 32, :]
            if d == 0:
                r = r * live_high
            if d == 1:
                r = r * live_low
            residues.append(r)
        step = omegas[k] * times_square(jnp.concatenate(residues, axis=0), mx_c[...])
        new = step + lam[c] if k > 0 else step
        lam[c] = new
        spread_traces(new, m, tx_out.at[c], ty_out.at[c])

    def move(c):
        arrived(0, c)
        update(0, c)
        sums, rows = [None, None], []
        q0j = planes[1]
        for i in range(N):
            add = table[1, i] * tx_out[c, i % 2] + q0j * ty_out[c, i : i + 1, :]
            reduce_one(g_out[c, i] * add, i, sums, rows)
        face_sums(*sums, y_scr[...], moduli[c], face.at[c], True)
        send_faces(1, c)

    def back(c):
        arrived(1, c)
        update(1, c)
        q0j = planes[1]
        for i in range(0, N, 2):
            values = []
            for n in range(2):
                add = table[1, i + n] * tx_out[c, n] + q0j * ty_out[c, i + n : i + n + 1, :]
                values.append(u_out[c, i + n] + g_out[c, i + n] * add)
            a, b = pair_y(lyi_c[...], *values)
            t_scr[pl.ds(i, 32, stride=STRIDE), :] = a
            t_scr[pl.ds(i + 1, 32, stride=STRIDE), :] = b
        x_either(t_scr, x_scr if c == 0 else x_out.at[c - 1], lx_c[...])
        if c == 0:
            for p in range(16):
                z_back(x_scr, o_out, wz_c[...], p)

    for c in range(COMPS):
        forward(c)
    for d in range(4):
        from_present(d, mcopy(d).wait_recv)
    for c in range(COMPS):
        move(c)
    for c in range(COMPS):
        back(c)
    for d in range(4):
        where_present(d, mcopy(d).wait_send)
    for k in range(ITERS):
        for c in range(COMPS):
            for d in range(4):
                where_present(d, gcopy(k, c, d).wait_send)


CHUNKS = 4


def back_kernel(x_ref, first_ref, wz_c, out_hbm, o_scr, out_sem, first_sem):
    def ocopy(c, chunk, side):
        first = chunk * 512 if side == 0 else 3584 - chunk * 512
        return pltpu.make_async_copy(
            o_scr.at[c, :, pl.ds(first, 512)],
            out_hbm.at[c + 1, :, pl.ds(first, 512)],
            out_sem.at[c, chunk, side],
        )

    whole = pltpu.make_async_copy(first_ref, out_hbm.at[0], first_sem)
    whole.start()
    for c in range(COMPS - 1):
        for chunk in range(CHUNKS):
            for p in range(4 * chunk, 4 * chunk + 4):
                z_back(x_ref.at[c], o_scr.at[c], wz_c[...], p)
            ocopy(c, chunk, 0).start()
            ocopy(c, chunk, 1).start()
    for c in range(COMPS - 1):
        for chunk in range(CHUNKS):
            ocopy(c, chunk, 0).wait()
            ocopy(c, chunk, 1).wait()
    whole.wait()


def shards(forcing, modulus, orient_codes):
    lx, ly, lyi, wz, mx, table, planes = (jnp.asarray(a) for a in constants())
    f = forcing.reshape(COMPS, N, N * N)
    vmem = pl.BlockSpec(memory_space=pltpu.VMEM)
    smem = pl.BlockSpec(memory_space=pltpu.SMEM)
    hbm = pl.BlockSpec(memory_space=pltpu.HBM)
    spectral = (COMPS, N, N // 2, 128)
    x_back, first = pl.pallas_call(
        trace_kernel,
        out_shape=[
            pltpu.VMEM((COMPS - 1, 32 * STRIDE, 128), F32),
            pltpu.VMEM((N, N * N), F32),
        ],
        in_specs=[hbm, hbm, smem] + [hbm] * 7,
        out_specs=[vmem] * 2,
        scratch_shapes=[
            pltpu.SMEM((1, 1, COMPS), F32),
            pltpu.SMEM(table.shape, F32),
            pltpu.VMEM(lx.shape, BF16),
            pltpu.VMEM(ly.shape, BF16),
            pltpu.VMEM(lyi.shape, BF16),
            pltpu.VMEM(wz.shape, BF16),
            pltpu.VMEM(mx.shape, BF16),
            pltpu.VMEM(planes.shape, F32),
            pltpu.VMEM(spectral, F32),
            pltpu.VMEM(spectral, F32),
            pltpu.VMEM((COMPS, 2, 32, 128), F32),
            pltpu.VMEM((COMPS, N, 128), F32),
            pltpu.VMEM((COMPS, N, N * N), F32),
            pltpu.VMEM((32 * STRIDE, 128), F32),
            pltpu.VMEM((32 * STRIDE, 128), F32),
            pltpu.VMEM((N, 128), F32),
            pltpu.VMEM((COMPS, 128, 128), F32),
            pltpu.VMEM((COMPS, 128, 128), F32),
            pltpu.VMEM((8, 128), F32),
            pltpu.VMEM((4, 8, 128), F32),
            pltpu.VMEM((ITERS, COMPS, 4, 32, 128), F32),
            pltpu.VMEM((ITERS, COMPS, 4, 32, 128), F32),
            pltpu.SemaphoreType.DMA((6,)),
            pltpu.SemaphoreType.DMA((8,)),
            pltpu.SemaphoreType.DMA((4,)),
            pltpu.SemaphoreType.DMA((4,)),
            pltpu.SemaphoreType.DMA((ITERS, COMPS, 4)),
            pltpu.SemaphoreType.DMA((ITERS, COMPS, 4)),
        ],
        compiler_params=pltpu.CompilerParams(
            collective_id=0, has_side_effects=True, vmem_limit_bytes=40 * 2**20
        ),
        cost_estimate=pl.CostEstimate(flops=2 * 10**9, bytes_accessed=3 * 2**20, transcendentals=0),
        name="traces",
    )(in_hbm(f), in_hbm(modulus), orient_codes, *(in_hbm(a) for a in (table, lx, ly, lyi, wz, mx, planes)))
    out = pl.pallas_call(
        back_kernel,
        out_shape=jax.ShapeDtypeStruct((COMPS, N, N * N), F32),
        in_specs=[vmem] * 3,
        out_specs=hbm,
        scratch_shapes=[
            pltpu.VMEM((COMPS - 1, N, N * N), F32),
            pltpu.SemaphoreType.DMA((COMPS - 1, CHUNKS, 2)),
            pltpu.SemaphoreType.DMA(()),
        ],
        compiler_params=pltpu.CompilerParams(vmem_limit_bytes=40 * 2**20),
        cost_estimate=pl.CostEstimate(flops=2 * 10**9, bytes_accessed=3 * 2**20, transcendentals=0),
        name="back",
    )(x_back, first, wz)
    return out.reshape(forcing.shape)


def solution(mesh):
    placed = (P("blk", "face", None, None, None), P("blk", "face", None), P("blk", "face"))
    return jax.shard_map(
        shards,
        mesh=mesh,
        in_specs=placed,
        out_specs=P("blk", "face", None, None, None),
        check_vma=False,
    )
```

```python
import functools
import math

import jax
import jax.numpy as jnp
import ml_dtypes
import numpy as np
from jax import lax
from jax.experimental import pallas as pl
from jax.experimental.pallas import tpu as pltpu
from jax.sharding import PartitionSpec as P

N = 64
ITERS = 2
COMPS = 3
STRIDE = 72
MESH = pl.DeviceIdType.MESH
F32 = jnp.float32
BF16 = jnp.bfloat16
mass_shift = 0.02
inject_scale = 2.0
traction_mix = 0.5
penalty_mix = 0.25
lower_edge = 0.3
upper_edge = 1.5


def in_hbm(a):
    return pltpu.with_memory_space_constraint(a, pltpu.HBM)


def split_np(a):
    a = np.asarray(a, np.float32)
    hi = a.astype(ml_dtypes.bfloat16)
    lo = (a - hi.astype(np.float32)).astype(ml_dtypes.bfloat16)
    return hi, lo


def rows3(a):
    hi, lo = split_np(a)
    return np.concatenate([hi, hi, lo], axis=1)


def square3(a):
    hi, lo = split_np(a)
    top = np.concatenate([hi, lo], axis=1)
    bottom = np.concatenate([hi, np.zeros_like(hi)], axis=1)
    return np.concatenate([top, bottom], axis=0)


def constants():
    n = np.arange(1, N + 1, dtype=np.float64)
    q = math.sqrt(2.0 / (N + 1)) * np.sin(math.pi * n[:, None] * n[None, :] / (N + 1))
    e = 2.0 - 2.0 * np.cos(math.pi * n / (N + 1))
    tangent = np.diag(np.full(N, -2.0)) + np.diag(np.ones(N - 1), 1) + np.diag(np.ones(N - 1), -1)
    tangent[0, 0] = tangent[-1, -1] = -1.0
    smooth = np.eye(N) + penalty_mix * (q @ tangent @ q)
    half = N // 2
    sign = (-1.0) ** np.arange(half)
    fold = np.block([[q, q], [q, -q]])
    even, odd = q[0::2, :half], q[1::2, :half] * sign[None, :]
    lx = rows3(q)
    ly = rows3(np.concatenate([even, odd], axis=0))
    lyi = rows3(np.concatenate([even.T, odd.T], axis=0))
    wz = square3(fold)
    mx = square3(np.kron(np.eye(2), smooth))
    normal = q[0] + traction_mix * (11.0 / 6.0 * q[0] - 3.0 * q[1] + 1.5 * q[2] - q[3] / 3.0)
    table = np.stack([normal, q[0], e]).astype(np.float32)
    spread = lambda v: np.repeat(v.reshape(half, 2), N, axis=1)
    planes = np.stack(
        [spread(normal), spread(q[0]), spread(e) + np.tile(e, 2)[None, :]]
    ).astype(np.float32)
    return lx, ly, lyi, wz, mx, table, planes


def step_weights():
    mid = 0.5 * (upper_edge + lower_edge)
    radius = 0.5 * (upper_edge - lower_edge)
    return [
        1.0 / (mid + radius * math.cos(math.pi * (2 * k + 1) / (2 * ITERS))) for k in range(ITERS)
    ]


def lane_iota():
    return lax.broadcasted_iota(jnp.int32, (1, 128), 1)


def split(a):
    hi = a.astype(BF16)
    lo = (a - hi.astype(F32)).astype(BF16)
    return hi, lo


def stack3(a):
    hi, lo = split(a)
    return jnp.concatenate([hi, lo, hi], axis=0)


def times_square(a, w):
    hi, lo = split(a)
    r = jnp.dot(jnp.concatenate([hi, lo], axis=1), w, preferred_element_type=F32)
    return r[:, :128] + r[:, 128:]


def dot(a, b):
    return jnp.dot(a, b, preferred_element_type=F32)


def row_at(y):
    return slice(y * STRIDE, y * STRIDE + N)


def z_forward(x_ref, t_ref, wz, steps):
    low = lane_iota() < N
    for p in steps:
        a = x_ref[:, p * 128 : p * 128 + 128]
        b = x_ref[:, (31 - p) * 128 : (32 - p) * 128]
        z = times_square(jnp.concatenate([jnp.where(low, a, b), jnp.where(low, b, a)], axis=0), wz)
        t_ref[row_at(2 * p), :] = z[:N]
        t_ref[row_at(2 * p + 1), :] = z[N:]


def x_either(a_ref, b_ref, lx):
    for p in range(16):
        a = jnp.concatenate([a_ref[row_at(2 * p), :], a_ref[row_at(2 * p + 1), :]], axis=1)
        r = dot(lx, stack3(a))
        b_ref[row_at(2 * p), :] = r[:, :128]
        b_ref[row_at(2 * p + 1), :] = r[:, 128:]


def z_back(t_ref, o_ref, wz, p):
    low = lane_iota() < N
    both = jnp.concatenate([t_ref[row_at(2 * p), :], t_ref[row_at(2 * p + 1), :]], axis=0)
    o = times_square(both, wz)
    a, b = o[:N], o[N:]
    o_ref[:, p * 128 : p * 128 + 128] = jnp.where(low, a, b)
    o_ref[:, (31 - p) * 128 : (32 - p) * 128] = jnp.where(low, b, a)


def pair_y(ly, a, b):
    low = lane_iota() < N
    r = dot(ly, stack3(jnp.concatenate([a, b], axis=1)))
    return (
        jnp.where(low, r[:32, :128], r[32:, :128]),
        jnp.where(low, r[:32, 128:], r[32:, 128:]),
    )


def orient_row(code):
    lane = lane_iota()
    rows = jnp.where(lane < N, 1.0, -1.0)
    cols = jnp.where(lane % 2 == 0, 1.0, -1.0)
    one = jnp.ones((1, 128), F32)
    return jnp.where(code % 2 == 1, rows, one) * jnp.where(code // 2 == 1, cols, one)


def face_sums(se, so, y, m, g_ref, add):
    low = lane_iota() < N
    swapped = pltpu.roll(y, N, 1)
    total, diff = y + swapped, y - swapped
    parts = [
        se - so,
        se + so,
        jnp.where(low, diff[:32], -diff[32:]),
        jnp.where(low, total[:32], total[32:]),
    ]
    for at, part in enumerate(parts):
        rows = slice(32 * at, 32 * at + 32)
        value = m * part
        g_ref[rows, :] = value + g_ref[rows, :] if add else value


def spread_traces(lam, m, lx_ref, ly_ref):
    low = lane_iota() < N
    scale = inject_scale * m
    xh, xl, yh, yl = (lam[32 * i : 32 * i + 32] for i in range(4))
    lx_ref[0] = scale * (xl + xh)
    lx_ref[1] = scale * (xl - xh)
    pe, po = scale * (yl + yh), scale * (yl - yh)
    ly_ref[0:32, :] = jnp.where(low, pe, pltpu.roll(po, N, 1))
    ly_ref[32:64, :] = jnp.where(low, pltpu.roll(pe, N, 1), po)


def trace_kernel(
    f_hbm, mod_h, codes, table_h, lx_h, ly_h, lyi_h, wz_h, mx_h, planes_h,
    x_out, o_out,
    mod, table, lx_c, ly_c, lyi_c, wz_c, mx_c, planes, u_out, g_out, tx_out, ty_out,
    xin, t_scr, x_scr, y_scr, face, lam, msend, mrecv, send, recv,
    in_sem, con_sem, msend_sem, mrecv_sem, send_sem, recv_sem,
):
    s, j = lax.axis_index("blk"), lax.axis_index("face")
    ns, nj = lax.axis_size("blk"), lax.axis_size("face")
    partner = [
        (lax.rem(s + ns - 1, ns), j),
        (lax.rem(s + 1, ns), j),
        (s, lax.rem(j + nj - 1, nj)),
        (s, lax.rem(j + 1, nj)),
    ]
    barrier = pltpu.get_barrier_semaphore()
    strips = [
        pltpu.make_async_copy(
            f_hbm.at[0, :, pl.ds(at * 1024, 1024)], xin.at[0, :, pl.ds(at * 1024, 1024)],
            in_sem.at[n],
        )
        for n, at in enumerate((0, 3, 1, 2))
    ]
    loads = [
        pltpu.make_async_copy(f_hbm.at[c], xin.at[c], in_sem.at[3 + c]) for c in range(1, COMPS)
    ]
    pairs = [
        (mod_h, mod), (table_h, table), (planes_h, planes),
        (wz_h, wz_c), (lx_h, lx_c), (ly_h, ly_c), (mx_h, mx_c), (lyi_h, lyi_c),
    ]
    small = [pltpu.make_async_copy(a, b, con_sem.at[i]) for i, (a, b) in enumerate(pairs)]
    strips[0].start()
    strips[1].start()
    for copy in small[:4]:
        copy.start()
    strips[2].start()
    strips[3].start()
    for copy in small[4:]:
        copy.start()
    for load in loads:
        load.start()
    recv[:, :, 0:2] = jnp.zeros((ITERS, COMPS, 2, 32, 128), F32)
    mrecv[0:2] = jnp.ones((2, 8, 128), F32)
    present = [s > 0, s < ns - 1, None, None]

    def where_present(d, action):
        if present[d] is None:
            action()
        else:
            pl.when(present[d])(action)

    def from_present(d, action):
        where_present(d ^ 1 if d < 2 else d, action)

    for d in range(4):
        where_present(
            d,
            lambda d=d: pl.semaphore_signal(
                barrier, inc=1, device_id=partner[d], device_id_type=MESH
            ),
        )

    for copy in small[:3]:
        copy.wait()
    row = lax.broadcasted_iota(jnp.int32, (8, 128), 0)
    moduli = [mod[0, 0, c] for c in range(COMPS)]
    msend[...] = jnp.where(row == 0, moduli[0], jnp.where(row == 1, moduli[1], moduli[2]))
    flip = orient_row(codes[0, 0])
    live_high = jnp.where(s < ns - 1, 1.0, 0.0).astype(F32)
    live_low = jnp.where(s > 0, 1.0, 0.0).astype(F32)
    omegas = step_weights()

    def gain(c, i):
        d = (moduli[c] * planes[2] + mass_shift) + moduli[c] * table[2, i]
        r = pl.reciprocal(d, approx=True)
        return r * (2.0 - d * r)

    def fill(i, carry):
        g_out[0, i] = gain(0, i)
        return carry

    lax.fori_loop(0, N, fill, 0, unroll=8)

    def mcopy(d):
        return pltpu.make_async_remote_copy(
            src_ref=msend, dst_ref=mrecv.at[d], send_sem=msend_sem.at[d],
            recv_sem=mrecv_sem.at[d], device_id=partner[d], device_id_type=MESH,
        )

    def gcopy(k, c, d):
        return pltpu.make_async_remote_copy(
            src_ref=send.at[k, c, d], dst_ref=recv.at[k, c, d], send_sem=send_sem.at[k, c, d],
            recv_sem=recv_sem.at[k, c, d], device_id=partner[d], device_id_type=MESH,
        )


    def send_faces(k, c):
        send[k, c, 0] = face[c, 32:64, :]
        send[k, c, 1] = face[c, 0:32, :] * flip
        send[k, c, 2] = face[c, 96:128, :]
        send[k, c, 3] = face[c, 64:96, :]
        for d in range(4):
            where_present(d, gcopy(k, c, d).start)

    def reduce_one(u, i, sums, rows):
        weighted = table[0, i] * u
        sums[i % 2] = weighted if sums[i % 2] is None else sums[i % 2] + weighted
        w = planes[0] * u
        rows.append((w[0:8] + w[8:16]) + (w[16:24] + w[24:32]))
        if len(rows) == 8:
            y_scr[i - 7 : i + 1, :] = jnp.sum(jnp.stack(rows, axis=0), axis=1)
            rows.clear()

    def forward(c):
        if c == 0:
            small[3].wait()
            strips[0].wait()
            strips[1].wait()
            z_forward(xin.at[c], t_scr, wz_c[...], range(8))
            strips[2].wait()
            strips[3].wait()
            z_forward(xin.at[c], t_scr, wz_c[...], range(8, 16))
            for copy in small[4:]:
                copy.wait()
        else:
            loads[c - 1].wait()
            z_forward(xin.at[c], t_scr, wz_c[...], range(16))
        x_either(t_scr, x_scr, lx_c[...])
        sums, rows = [None, None], []
        for first in range(0, N, 2):
            a = x_scr[pl.ds(first, 32, stride=STRIDE), :]
            b = x_scr[pl.ds(first + 1, 32, stride=STRIDE), :]
            for i, h in zip((first, first + 1), pair_y(ly_c[...], a, b)):
                g = g_out[0, i] if c == 0 else gain(c, i)
                if c > 0:
                    g_out[c, i] = g
                u = h * g
                u_out[c, i] = u
                reduce_one(u, i, sums, rows)
        face_sums(*sums, y_scr[...], moduli[c], face.at[c], False)
        if c == 0:
            pl.semaphore_wait(barrier, 4 - jnp.where(s > 0, 0, 1) - jnp.where(s < ns - 1, 0, 1))
            for d in range(4):
                where_present(d, mcopy(d).start)
        send_faces(0, c)

    def arrived(k, c):
        for d in range(4):
            from_present(d, gcopy(k, c, d).wait_recv)

    def update(k, c):
        m = moduli[c]
        order = [0, 1, 2, 3]
        residues = []
        for at, d in enumerate(order):
            other = recv[k, c, d]
            if d == 0:
                other = other * flip
            inverse = 1.0 / (m + mrecv[d, c : c + 1, :])
            r = (face[c, 32 * at : 32 * at + 32, :] + other) * inverse
            if k > 0:
                r = r - lam[c, 32 * at : 32 * at + 32, :]
            if d == 0:
                r = r * live_high
            if d == 1:
                r = r * live_low
            residues.append(r)
        step = omegas[k] * times_square(jnp.concatenate(residues, axis=0), mx_c[...])
        new = step + lam[c] if k > 0 else step
        lam[c] = new
        spread_traces(new, m, tx_out.at[c], ty_out.at[c])

    def move(c):
        arrived(0, c)
        update(0, c)
        sums, rows = [None, None], []
        q0j = planes[1]
        for i in range(N):
            add = table[1, i] * tx_out[c, i % 2] + q0j * ty_out[c, i : i + 1, :]
            reduce_one(g_out[c, i] * add, i, sums, rows)
        face_sums(*sums, y_scr[...], moduli[c], face.at[c], True)
        send_faces(1, c)

    def back(c):
        if c != 1:
            arrived(1, c)
            update(1, c)
        q0j = planes[1]
        for i in range(0, N, 2):
            values = []
            for n in range(2):
                add = table[1, i + n] * tx_out[c, n] + q0j * ty_out[c, i + n : i + n + 1, :]
                values.append(u_out[c, i + n] + g_out[c, i + n] * add)
            a, b = pair_y(lyi_c[...], *values)
            t_scr[pl.ds(i, 32, stride=STRIDE), :] = a
            t_scr[pl.ds(i + 1, 32, stride=STRIDE), :] = b
        x_either(t_scr, x_scr if c == 0 else x_out.at[c - 1], lx_c[...])
        if c == 0:
            arrived(1, 1)
            update(1, 1)
            for p in range(16):
                z_back(x_scr, o_out, wz_c[...], p)

    for c in range(COMPS):
        forward(c)
    for d in range(4):
        from_present(d, mcopy(d).wait_recv)
    for c in range(COMPS):
        move(c)
    for c in range(COMPS):
        back(c)
    for d in range(4):
        where_present(d, mcopy(d).wait_send)
    for k in range(ITERS):
        for c in range(COMPS):
            for d in range(4):
                where_present(d, gcopy(k, c, d).wait_send)


CHUNKS = 4


def back_kernel(x_ref, first_ref, wz_c, out_hbm, o_scr, out_sem, first_sem):
    def ocopy(c, chunk, side):
        first = chunk * 512 if side == 0 else 3584 - chunk * 512
        return pltpu.make_async_copy(
            o_scr.at[c, :, pl.ds(first, 512)],
            out_hbm.at[c + 1, :, pl.ds(first, 512)],
            out_sem.at[c, chunk, side],
        )

    whole = pltpu.make_async_copy(first_ref, out_hbm.at[0], first_sem)
    whole.start()
    for c in range(COMPS - 1):
        for chunk in range(CHUNKS):
            for p in range(4 * chunk, 4 * chunk + 4):
                z_back(x_ref.at[c], o_scr.at[c], wz_c[...], p)
            ocopy(c, chunk, 0).start()
            ocopy(c, chunk, 1).start()
    for c in range(COMPS - 1):
        for chunk in range(CHUNKS):
            ocopy(c, chunk, 0).wait()
            ocopy(c, chunk, 1).wait()
    whole.wait()


def shards(forcing, modulus, orient_codes):
    lx, ly, lyi, wz, mx, table, planes = (jnp.asarray(a) for a in constants())
    f = forcing.reshape(COMPS, N, N * N)
    vmem = pl.BlockSpec(memory_space=pltpu.VMEM)
    smem = pl.BlockSpec(memory_space=pltpu.SMEM)
    hbm = pl.BlockSpec(memory_space=pltpu.HBM)
    spectral = (COMPS, N, N // 2, 128)
    x_back, first = pl.pallas_call(
        trace_kernel,
        out_shape=[
            pltpu.VMEM((COMPS - 1, 32 * STRIDE, 128), F32),
            pltpu.VMEM((N, N * N), F32),
        ],
        in_specs=[hbm, hbm, smem] + [hbm] * 7,
        out_specs=[vmem] * 2,
        scratch_shapes=[
            pltpu.SMEM((1, 1, COMPS), F32),
            pltpu.SMEM(table.shape, F32),
            pltpu.VMEM(lx.shape, BF16),
            pltpu.VMEM(ly.shape, BF16),
            pltpu.VMEM(lyi.shape, BF16),
            pltpu.VMEM(wz.shape, BF16),
            pltpu.VMEM(mx.shape, BF16),
            pltpu.VMEM(planes.shape, F32),
            pltpu.VMEM(spectral, F32),
            pltpu.VMEM(spectral, F32),
            pltpu.VMEM((COMPS, 2, 32, 128), F32),
            pltpu.VMEM((COMPS, N, 128), F32),
            pltpu.VMEM((COMPS, N, N * N), F32),
            pltpu.VMEM((32 * STRIDE, 128), F32),
            pltpu.VMEM((32 * STRIDE, 128), F32),
            pltpu.VMEM((N, 128), F32),
            pltpu.VMEM((COMPS, 128, 128), F32),
            pltpu.VMEM((COMPS, 128, 128), F32),
            pltpu.VMEM((8, 128), F32),
            pltpu.VMEM((4, 8, 128), F32),
            pltpu.VMEM((ITERS, COMPS, 4, 32, 128), F32),
            pltpu.VMEM((ITERS, COMPS, 4, 32, 128), F32),
            pltpu.SemaphoreType.DMA((6,)),
            pltpu.SemaphoreType.DMA((8,)),
            pltpu.SemaphoreType.DMA((4,)),
            pltpu.SemaphoreType.DMA((4,)),
            pltpu.SemaphoreType.DMA((ITERS, COMPS, 4)),
            pltpu.SemaphoreType.DMA((ITERS, COMPS, 4)),
        ],
        compiler_params=pltpu.CompilerParams(
            collective_id=0, has_side_effects=True, vmem_limit_bytes=40 * 2**20
        ),
        cost_estimate=pl.CostEstimate(flops=2 * 10**9, bytes_accessed=3 * 2**20, transcendentals=0),
        name="traces",
    )(in_hbm(f), in_hbm(modulus), orient_codes, *(in_hbm(a) for a in (table, lx, ly, lyi, wz, mx, planes)))
    out = pl.pallas_call(
        back_kernel,
        out_shape=jax.ShapeDtypeStruct((COMPS, N, N * N), F32),
        in_specs=[vmem] * 3,
        out_specs=hbm,
        scratch_shapes=[
            pltpu.VMEM((COMPS - 1, N, N * N), F32),
            pltpu.SemaphoreType.DMA((COMPS - 1, CHUNKS, 2)),
            pltpu.SemaphoreType.DMA(()),
        ],
        compiler_params=pltpu.CompilerParams(vmem_limit_bytes=40 * 2**20),
        cost_estimate=pl.CostEstimate(flops=2 * 10**9, bytes_accessed=3 * 2**20, transcendentals=0),
        name="back",
    )(x_back, first, wz)
    return out.reshape(forcing.shape)


def solution(mesh):
    placed = (P("blk", "face", None, None, None), P("blk", "face", None), P("blk", "face"))
    return jax.shard_map(
        shards,
        mesh=mesh,
        in_specs=placed,
        out_specs=P("blk", "face", None, None, None),
        check_vma=False,
    )
```
